32 devices in a mesh: section: 2 (over y), pb: 8 (over z, core), fsdp: 2 (over x).
Axes of the slice: x: 2, y: 2, z: 4, core: 2. Of those that a mesh axis runs over, the one named last changes fastest.
Arguments:
- decoder_states: bfloat16 [8, 32, 4096], P('pb', None, 'fsdp'), may hold values from -90 to 90
- norm_gain: bfloat16 [4096], P('fsdp'), may hold values from 0.099609375 to 1.8984375
- query_weight: bfloat16 [4096, 2048], P('fsdp', 'section'), may hold values from -0.046875 to 0.046875
- key_weight: bfloat16 [4096, 2048], P(('pb', 'fsdp'), 'section'), may hold values from -0.09375 to 0.09375
- value_weight: bfloat16 [4096, 2048], P(('pb', 'fsdp'), 'section'), may hold values from -0.09375 to 0.09375
- out_weight: bfloat16 [2048, 4096], P('section', 'fsdp'), may hold values from -0.5 to 0.5
- passage_states: bfloat16 [8, 2048, 4096], P('fsdp', 'pb'), may hold values from -400 to 400
- block_mask: int32 [8, 16], replicated, may hold values from 0 to 1, as said below
Outputs:
- cross_out: bfloat16 [8, 32, 4096], P('pb', None, 'fsdp')
The draws below stay inside these ranges and needn't reach their ends.
Inputs may be any that keep to these rules, and one draw needn't show every extreme that they name: `block_mask`: every question has at least one live block.
All inputs are finite; a program needn't handle non-finite values.
Results may differ from the reference program's by a relative error of at most 0.01.
The reference program's roundings to bfloat16 on the way (of `scaled`, `query`, `keys`, `values`, `weights` and `attention`) count: a program that leaves them out, or rounds other values in their place, can miss the bound.
Values may be sent and summed in bfloat16 or wider, within the bound.
No kernel may reach another device: no remote copies, remote signals or barrier semaphores. Data moves between devices by JAX's collectives and lax.ppermute only.
A program may use at most 128 MiB of HBM per device.

```python
import jax
import jax.numpy as jnp
from jax import lax

D = 4096
HD = 64
HEADS = 32
ANSWER = 32
BLOCK = 128
INNER = 2048
QUESTIONS = 8
ROWS = 2048
BLOCKS = 16


def draw_decoder_states(key, part):
    base = jnp.clip(jax.random.normal(jax.random.fold_in(key, 1), (QUESTIONS, ANSWER, D), jnp.float32), -5.0, 5.0)
    column = 0.5 + jnp.arange(D, dtype=jnp.float32) / D
    return (base * column[None, None, :]).astype(jnp.bfloat16)


def draw_passage_states(key, part):
    base = jnp.clip(jax.random.normal(jax.random.fold_in(key, 4), (QUESTIONS, ROWS, D), jnp.float32), -5.0, 5.0)
    return base.astype(jnp.bfloat16)


def draw_block_mask(key, part):
    level = jax.random.randint(jax.random.fold_in(key, 11), (QUESTIONS, 1), 1, 9)
    ticket = jax.random.randint(jax.random.fold_in(key, 12), (QUESTIONS, BLOCKS), 0, 8)
    forced = jax.random.randint(jax.random.fold_in(key, 13), (QUESTIONS, 1), 0, BLOCKS)
    places = jnp.arange(BLOCKS, dtype=jnp.int32)[None, :]
    live_flags = (ticket < level) | (places == forced)
    return live_flags.astype(jnp.int32)


def level_of(stream_key, dims, shards, smallest, high):
    factor_of, own = 1.0, jax.random.fold_in(stream_key, 6)
    for axis_at, parts in shards:
        draws = jnp.exp(jax.random.uniform(jax.random.fold_in(own, axis_at), (parts,), jnp.float32, smallest / len(shards), high / len(shards)))
        factor_of = factor_of * jnp.repeat(draws, dims[axis_at] // parts).reshape([-1 if axis == axis_at else 1 for axis in range(len(dims))])
    return factor_of


def centred(key, shape, spread, most, split=(), kind=jnp.bfloat16):
    drawn = spread * jax.random.normal(key, shape, jnp.float32)
    if split:
        drawn = drawn * level_of(key, shape, split, -0.22, 0.18)
    return jnp.clip(drawn, -most, most).astype(kind)


def setup_inputs(seed: int = 0) -> dict:
    key_list = jax.random.split(jax.random.key(seed), 9)
    return {
        "decoder_states": draw_decoder_states(jax.random.fold_in(key_list[8], 71), 0),
        "norm_gain": jnp.clip(1.0 + 0.18 * jax.random.normal(key_list[1], (D,), jnp.float32), 0.099609375, 1.8984375).astype(jnp.bfloat16),
        "query_weight": centred(key_list[2], (D, INNER), (4 * D) ** -0.5, 0.046875, ((0, 2), (1, 2))),
        "key_weight": centred(key_list[3], (D, INNER), D ** -0.5, 0.09375, ((0, 16), (1, 2))),
        "value_weight": centred(key_list[4], (D, INNER), D ** -0.5, 0.09375, ((0, 16), (1, 2))),
        "out_weight": centred(key_list[5], (INNER, D), (INNER // 16) ** -0.5, 0.5, ((0, 2), (1, 2))),
        "passage_states": draw_passage_states(jax.random.fold_in(key_list[8], 71), 0),
        "block_mask": draw_block_mask(jax.random.fold_in(key_list[8], 71), 0),
    }


NEGATIVE = -1e+30

def rounded(value):
    return lax.optimization_barrier(value.astype(jnp.bfloat16))

def reference(decoder_states, norm_gain, query_weight, key_weight, value_weight, out_weight, passage_states, block_mask):
    states_wide = decoder_states.astype(jnp.float32)
    square_mean = lax.optimization_barrier(jnp.mean(states_wide * states_wide, axis=2))
    scaled = rounded(states_wide * norm_gain.astype(jnp.float32)[None, None, :])
    query_raw = jnp.einsum('qad,de->qae', scaled.astype(jnp.float32), query_weight.astype(jnp.float32))
    query = (query_raw * lax.rsqrt(square_mean + 1e-06)[:, :, None]).astype(jnp.bfloat16)
    row_live = jnp.repeat(block_mask, BLOCK, axis=1) > 0

    def one_question(packed):
        passages, question, visible = packed
        keys = rounded(jnp.dot(passages, key_weight, preferred_element_type=jnp.float32))
        values = rounded(jnp.dot(passages, value_weight, preferred_element_type=jnp.float32))
        queries = question.reshape(ANSWER, HEADS, HD).astype(jnp.float32)
        keys_split = keys.reshape(ROWS, HEADS, HD).astype(jnp.float32)
        values_split = values.reshape(ROWS, HEADS, HD).astype(jnp.float32)
        scores = jnp.einsum('ahd,rhd->ahr', queries, keys_split)
        shown = visible[None, None, :]
        scores = jnp.where(shown, scores, NEGATIVE)
        peak = lax.optimization_barrier(jnp.max(scores, axis=2, keepdims=True))
        raw_weights = jnp.where(shown, jnp.exp(scores - peak), 0.0)
        totals = lax.optimization_barrier(jnp.sum(raw_weights, axis=2, keepdims=True))
        weights = rounded(raw_weights)
        numerator = jnp.einsum('ahr,rhd->ahd', weights.astype(jnp.float32), values_split)
        attention = (numerator / totals).astype(jnp.bfloat16).reshape(ANSWER, INNER)
        return jnp.dot(attention, out_weight, preferred_element_type=jnp.float32).astype(jnp.bfloat16)
    return lax.map(one_question, (passage_states, query, row_live))
```

```python
import functools

import jax
import jax.numpy as jnp
from jax import lax
from jax.experimental import pallas as pl
from jax.experimental.pallas import tpu as pltpu
from jax.sharding import PartitionSpec as P

HD = 64
BLOCK = 128
PASSAGE = 256


NEGATIVE = -1e30


def joined(value, axis, combine):
    everything = jax.tree.map(lambda part: lax.all_gather(part, axis), value)
    leading = jax.tree.map(lambda part: part[0], everything)

    def turn(k, so_far):
        return combine(so_far, jax.tree.map(lambda part: part[k], everything))

    return lax.fori_loop(1, lax.axis_size(axis), turn, leading)


def pack_order(alive_flags):
    amount = alive_flags.shape[0]
    ahead_count = jnp.cumsum(alive_flags) - alive_flags
    behind = jnp.cumsum(1 - alive_flags) - (1 - alive_flags)
    filled = jnp.sum(alive_flags)
    slot_index = jnp.where(alive_flags > 0, ahead_count, filled + behind)
    places = jnp.arange(amount, dtype=jnp.int32)
    order_index = jnp.sum(
        jnp.where(slot_index[None, :] == places[:, None], places[None, :], 0), axis=1
    )
    return (slot_index, order_index, filled)


def project(pieces, alive_flags, stacked):
    amount, piece_rows, model_width = pieces.shape
    slot_index, order_index, filled = pack_order(alive_flags)
    packed = pieces[order_index]
    per_group = min(amount, max(1, 256 // piece_rows))
    columns = stacked.shape[1]

    def compute(row_block):
        return jnp.dot(row_block, stacked, preferred_element_type=jnp.float32).astype(jnp.bfloat16)

    def skipped(row_block):
        return jnp.zeros((row_block.shape[0], columns), jnp.bfloat16)

    def advance(group_index, buffer):
        first_piece = group_index * per_group
        row_block = lax.dynamic_slice_in_dim(packed, first_piece, per_group, 0).reshape(
            per_group * piece_rows, model_width
        )
        result = lax.cond(first_piece < filled, compute, skipped, row_block)
        return lax.dynamic_update_slice_in_dim(
            buffer, result.reshape(per_group, piece_rows, columns), first_piece, 0
        )

    empty_buffer = jnp.zeros((amount, piece_rows, columns), jnp.bfloat16)
    buffer = lax.fori_loop(0, amount // per_group, advance, empty_buffer)
    return (buffer, slot_index, filled)


def attend(query, keyval, live_rows):
    row_total, doubled = keyval.shape
    half_width = doubled // 2
    head_count = half_width // HD
    answer_len = query.shape[0]
    keys_part = keyval[:, :half_width].reshape(row_total, head_count, HD)
    values_part = keyval[:, half_width:].reshape(row_total, head_count, HD)
    queries = query.reshape(answer_len, head_count, HD)
    scores = jnp.einsum("ahd,rhd->ahr", queries, keys_part, preferred_element_type=jnp.float32)
    shown = live_rows[None, None, :]
    scores = jnp.where(shown, scores, NEGATIVE)
    peak = jnp.max(scores, axis=2)
    raw_weights = jnp.where(shown, jnp.exp(scores - peak[:, :, None]), 0.0)
    totals = jnp.sum(raw_weights, axis=2)
    numerator = jnp.einsum(
        "ahr,rhd->ahd",
        raw_weights.astype(jnp.bfloat16),
        values_part,
        preferred_element_type=jnp.float32,
    )
    return (peak, totals, numerator)


def combine_parts(first, second):
    peak_one, totals_one, numer_one = first
    peak_two, totals_two, numer_two = second
    peak = jnp.maximum(peak_one, peak_two)
    factor_one = jnp.exp(peak_one - peak)
    factor_two = jnp.exp(peak_two - peak)
    totals = totals_one * factor_one + totals_two * factor_two
    numerator = numer_one * factor_one[:, :, None] + numer_two * factor_two[:, :, None]
    return (peak, totals, numerator)


def plain_shards(
    decoder_states,
    norm_gain,
    query_weight,
    key_weight,
    value_weight,
    out_weight,
    passage_states,
    block_mask,
):
    pb_count = lax.axis_size("pb")
    fsdp_count = lax.axis_size("fsdp")
    pb_index = lax.axis_index("pb")
    fsdp_index = lax.axis_index("fsdp")
    local_questions, local_rows, model_width = passage_states.shape
    block_total = block_mask.shape[1]
    passages_here = local_rows // PASSAGE
    piece_rows = PASSAGE // fsdp_count
    block_ids = jnp.arange(block_total, dtype=jnp.int32)
    own_mask = lax.dynamic_slice_in_dim(block_mask, pb_index, 1, 0)[0]
    passage_ids = jnp.arange(pb_count * passages_here, dtype=jnp.int32)
    piece_block = (passage_ids * PASSAGE + fsdp_index * piece_rows) // BLOCK
    decoder_live = jnp.sum(
        jnp.where(piece_block[:, None] == block_ids[None, :], own_mask[None, :], 0), axis=1
    )
    stacked_local = jnp.concatenate([key_weight, value_weight], axis=1)
    stacked = lax.all_gather(stacked_local, ("pb", "fsdp"), axis=0, tiled=True)
    own_states = decoder_states[0]
    states_wide = own_states.astype(jnp.float32)
    square_part = jnp.sum(states_wide * states_wide, axis=1)
    scaled = (states_wide * norm_gain.astype(jnp.float32)[None, :]).astype(jnp.bfloat16)
    query_part = jnp.dot(scaled, query_weight, preferred_element_type=jnp.float32)
    square_sum, query_raw = lax.psum((square_part, query_part), "fsdp")
    query = (query_raw * lax.rsqrt(square_sum / model_width + 1e-06)[:, None]).astype(jnp.bfloat16)
    shaped = passage_states.reshape(
        local_questions, passages_here, fsdp_count, piece_rows, model_width
    )
    by_piece = lax.all_to_all(shaped, "fsdp", split_axis=2, concat_axis=0, tiled=True)
    by_question = lax.all_to_all(by_piece, "pb", split_axis=0, concat_axis=1, tiled=True)
    pieces = by_question.reshape(pb_count * passages_here, piece_rows, model_width)
    projected, slot_index, filled = project(pieces, decoder_live, stacked)
    keyval = projected.reshape(pb_count * passages_here * piece_rows, projected.shape[2])
    live_rows = jnp.repeat(passage_ids < filled, piece_rows)
    peak, totals, numerator = attend(query, keyval, live_rows)
    peak, totals, numerator = joined((peak, totals, numerator), "fsdp", combine_parts)
    attention = (
        (numerator / totals[:, :, None])
        .astype(jnp.bfloat16)
        .reshape(query.shape[0], query.shape[1])
    )
    partial_out = jnp.dot(attention, out_weight, preferred_element_type=jnp.float32)
    summed_out = lax.psum(partial_out.astype(jnp.bfloat16), "section")
    return summed_out[None]


CHIPS = 4
PIECE = 256


def line(step, sources):
    return [(2 * z + c, 2 * (z + step) + c) for z in sources for c in range(2)]


def after(values, done):
    return lax.optimization_barrier((tuple(values), tuple(done)))[0]


def by_chip(z, options):
    picked = options[0]
    for place in range(1, CHIPS):
        if options[place] is not picked:
            picked = jnp.where(z >= place, options[place], picked)
    return picked


def core_swap(value):
    return lax.ppermute(value, "pb", [(p, p ^ 1) for p in range(2 * CHIPS)])


def gather_pieces(own, partner, z):
    def left(value, sources):
        return lax.ppermute(value, "pb", line(-1, sources))

    def right(value, sources):
        return lax.ppermute(value, "pb", line(1, sources))

    def across(value):
        return lax.ppermute(value, "fsdp", [(0, 1), (1, 0)])

    l_a1, r_a1, x_b = left(own, (1, 2, 3)), right(own, (0, 1, 2)), across(partner)
    l_b1, r_b1, x_a = left(partner, (1, 2, 3)), right(partner, (0, 1, 2)), across(own)

    l_a1, r_a1 = after((l_a1, r_a1), (x_b,))
    a1 = jnp.where(z < 2, l_a1, r_a1)
    l_a2, r_a2, x_a1 = left(l_a1, (1, 2)), right(r_a1, (1, 2)), across(a1)

    l_b1, r_b1, x_b = after((l_b1, r_b1, x_b), (x_a,))
    b1 = jnp.where(z < 2, l_b1, r_b1)
    l_b2 = left(jnp.where(z == 3, x_b, l_b1), (1, 2, 3))
    r_b2 = right(jnp.where(z == 0, x_b, r_b1), (0, 1, 2))
    x_b1 = across(b1)

    l_a2, r_a2 = after((l_a2, r_a2), (x_a1,))
    a2 = by_chip(z, (l_a2, r_a1, l_a1, r_a2))
    l_a3, r_a3, x_a2 = left(l_a2, (1,)), right(r_a2, (2,)), across(a2)

    l_b2, r_b2 = after((l_b2, r_b2), (x_b1,))
    l_b3, r_b3 = left(l_b2, (1, 2)), right(r_b2, (1, 2))
    ends = [(4 * k + 2 * c + x, 4 * k + 2 * c + 1 - x) for k in (0, 3) for c in range(2) for x in range(2)]
    x_b2 = lax.ppermute(jnp.where(z == 0, l_b2, r_b2), ("pb", "fsdp"), ends)

    l_a3, r_a3 = after((l_a3, r_a3), (x_a2,))
    a3 = by_chip(z, (l_a3, l_a2, r_a2, r_a3))
    x_a3 = across(a3)

    l_b3, r_b3 = after((l_b3, r_b3), (x_b2,))
    l_b4, r_b4 = left(l_b3, (1,)), right(r_b3, (2,))

    here = (0, 1, 2, 3)
    early = [
        ((own,) * 4, here, 0, 0),
        ((partner,) * 4, here, 0, 1),
        ((x_a,) * 4, here, 1, 0),
        ((x_b,) * 4, here, 1, 1),
        ((a1,) * 4, (1, 2, 1, 2), 0, 0),
        ((b1,) * 4, (1, 2, 1, 2), 0, 1),
        ((x_a1,) * 4, (1, 2, 1, 2), 1, 0),
        ((x_b1,) * 4, (1, 2, 1, 2), 1, 1),
        ((a2,) * 4, (2, 0, 3, 1), 0, 0),
        ((l_b2, r_b1, l_b1, r_b2), (2, 0, 3, 1), 0, 1),
    ]
    later = [
        ((a3,) * 4, (3, 3, 0, 0), 0, 0),
        ((l_b3, l_b2, r_b2, r_b3), (3, 3, 0, 0), 0, 1),
        ((x_a2,) * 4, (2, 0, 3, 1), 1, 0),
        ((x_b2, r_b2, l_b2, x_b2), (2, 0, 3, 1), 1, 1),
    ]
    last = [
        ((x_a3,) * 4, (3, 3, 0, 0), 1, 0),
        ((l_b4, l_b3, r_b3, r_b4), (3, 3, 0, 0), 1, 1),
    ]
    return early, later, last


def feature_blocks(pieces, z, c, f):
    found = []
    for _, origins, other_x, other_core in pieces:
        origin = by_chip(z, [jnp.int32(o) for o in origins])
        core = 1 - c if other_core else c
        place = 1 - f if other_x else f
        found.append(4 * origin + 2 * core + place)
    return jnp.stack(found)


def distinct(pieces):
    arrays, wanted = [], []
    for options, _, _, _ in pieces:
        spots = []
        for option in options:
            at = next((k for k, seen in enumerate(arrays) if seen is option), None)
            if at is None:
                at = len(arrays)
                arrays.append(option)
            spots.append(at)
        wanted.append(spots)
    return arrays, wanted


def load_weights(wanted, z, sources, weights, sems):
    for slot, spots in enumerate(wanted):
        target = weights.at[pl.ds(slot * PIECE, PIECE)]
        for at in sorted(set(spots)):
            zs = [k for k, spot in enumerate(spots) if spot == at]

            def begin(at=at, slot=slot, target=target):
                pltpu.make_async_copy(sources[at], target, sems.at[slot]).start()

            if len(zs) == CHIPS:
                begin()
            else:
                hit = functools.reduce(jnp.logical_or, [z == k for k in zs])
                pl.when(hit)(begin)
    for slot, spots in enumerate(wanted):
        target = weights.at[pl.ds(slot * PIECE, PIECE)]
        pltpu.make_async_copy(sources[spots[0]], target, sems.at[slot]).wait()


def project_kernel(wanted, amount, carried, info, own_rows, other_rows, *refs):
    refs = list(refs)
    before = refs.pop(0) if carried else None
    sources, (total, weights, sems) = refs[:amount], refs[amount:]
    count = len(wanted)

    @pl.when(pl.program_id(0) == 0)
    def _():
        load_weights(wanted, info[0], sources, weights, sems)

    for half, rows in enumerate((own_rows, other_rows)):
        here = pl.ds(half * rows.shape[1], rows.shape[1])
        features = jnp.concatenate(
            [rows[0, :, pl.ds(pl.multiple_of(info[1 + k] * PIECE, PIECE), PIECE)] for k in range(count)],
            axis=1,
        )
        part = jnp.dot(features, weights[...], preferred_element_type=jnp.float32)
        if carried:
            part = part + before[0, here, :]
        total[0, here, :] = part


def project_pieces(info, pieces, own_rows, other_rows, before=None):
    questions, rows, width = own_rows.shape
    columns = pieces[0][0][0].shape[1]
    arrays, wanted = distinct(pieces)
    count = len(pieces)
    carried = before is not None
    block = pl.BlockSpec((1, rows, width), lambda i, info: (i, 0, 0))
    sums = pl.BlockSpec((1, 2 * rows, columns), lambda i, info: (i, 0, 0))
    anywhere = pl.BlockSpec(memory_space=pl.ANY)
    flops = 2 * questions * 2 * rows * count * PIECE * columns
    return pl.pallas_call(
        functools.partial(project_kernel, wanted, len(arrays), carried),
        grid_spec=pltpu.PrefetchScalarGridSpec(
            num_scalar_prefetch=1,
            grid=(questions,),
            in_specs=[block, block] + ([sums] if carried else []) + [anywhere] * len(arrays),
            out_specs=sums,
            scratch_shapes=[
                pltpu.VMEM((count * PIECE, columns), jnp.bfloat16),
                pltpu.SemaphoreType.DMA((count,)),
            ],
        ),
        out_shape=jax.ShapeDtypeStruct((questions, 2 * rows, columns), jnp.float32),
        input_output_aliases={3: 0} if carried else {},
        compiler_params=pltpu.CompilerParams(vmem_limit_bytes=48 * 2**20),
        cost_estimate=pl.CostEstimate(
            flops=flops, bytes_accessed=questions * rows * (4 * width + 8 * columns), transcendentals=0
        ),
        name="project",
    )(info, own_rows, other_rows, *([before] if carried else []), *arrays)


def attend_kernel(wanted, amount, info, *refs):
    refs = list(refs)
    count = len(wanted)
    own_blocks, other_blocks, refs = refs[:count], refs[count : 2 * count], refs[2 * count :]
    before, queries, live, refs = refs[0], refs[1], refs[2], refs[3:]
    sources, refs = refs[:amount], refs[amount:]
    outs, (weights, sems) = refs[:CHIPS], refs[CHIPS:]
    step = pl.program_id(0)

    @pl.when(step == 0)
    def _():
        load_weights(wanted, info[0], sources, weights, sems)

    halves = []
    for half, blocks in enumerate((own_blocks, other_blocks)):
        rows = blocks[0].shape[1]
        features = jnp.concatenate([block[0] for block in blocks], axis=1)
        part = jnp.dot(features, weights[...], preferred_element_type=jnp.float32)
        halves.append((part + before[0, pl.ds(half * rows, rows), :]).astype(jnp.bfloat16))
    keyval = jnp.concatenate(halves, axis=0)
    width = keyval.shape[1] // 2
    answers = queries.shape[1]
    group = 4
    span = group * HD
    shown = live[0] > 0
    lane_head = lax.broadcasted_iota(jnp.int32, (answers, span), 1) // HD
    tail_lane = lax.broadcasted_iota(jnp.int32, (answers, 128), 1)
    head_total = width // HD
    extra = jnp.zeros((answers, 128), jnp.float32)
    parts = []
    for g in range(width // span):
        at = slice(g * span, (g + 1) * span)
        query = queries[0, :, at]
        spread = jnp.concatenate(
            [jnp.where(lane_head == h, query, jnp.zeros_like(query)) for h in range(group)], axis=0
        )
        scores = lax.dot_general(
            spread, keyval[:, at], (((1,), (1,)), ((), ())), preferred_element_type=jnp.float32
        )
        scores = jnp.where(shown, scores, NEGATIVE)
        peak = jnp.max(scores, axis=1, keepdims=True)
        raw = jnp.where(shown, jnp.exp(scores - peak), 0.0)
        total = jnp.sum(raw, axis=1, keepdims=True)
        value_at = slice(width + g * span, width + (g + 1) * span)
        numer = jnp.dot(raw.astype(jnp.bfloat16), keyval[:, value_at], preferred_element_type=jnp.float32)
        own = jnp.zeros((answers, span), jnp.float32)
        for h in range(group):
            mine = slice(h * answers, (h + 1) * answers)
            own = jnp.where(lane_head == h, numer[mine], own)
            extra = jnp.where(tail_lane == g * group + h, peak[mine], extra)
            extra = jnp.where(tail_lane == head_total + g * group + h, total[mine], extra)
        parts.append(own)
    result = jnp.concatenate(parts + [extra], axis=1)
    for k, out in enumerate(outs):

        @pl.when(step == k)
        def _(out=out):
            out[...] = result


def attend_last(info, pieces, own_rows, other_rows, before, queries, live):
    questions, rows, width = own_rows.shape
    columns = pieces[0][0][0].shape[1]
    answers = queries.shape[1]
    arrays, wanted = distinct(pieces)
    count = len(pieces)
    wide = columns // 2 + 128

    def question(i, info):
        return lax.rem(i + info[0], questions)

    blocks = [
        pl.BlockSpec((1, rows, PIECE), lambda i, info, k=k: (question(i, info), 0, info[1 + k]))
        for k in range(count)
    ]
    whole = lambda *shape: pl.BlockSpec((1,) + shape, lambda i, info: (question(i, info), 0, 0))
    anywhere = pl.BlockSpec(memory_space=pl.ANY)
    flops = 4 * questions * rows * count * PIECE * columns + 16 * questions * rows * answers * columns
    return pl.pallas_call(
        functools.partial(attend_kernel, wanted, len(arrays)),
        grid_spec=pltpu.PrefetchScalarGridSpec(
            num_scalar_prefetch=1,
            grid=(questions,),
            in_specs=blocks
            + blocks
            + [whole(2 * rows, columns), whole(answers, columns // 2), whole(1, 2 * rows)]
            + [anywhere] * len(arrays),
            out_specs=[pl.BlockSpec((answers, wide), lambda i, info: (0, 0))] * CHIPS,
            scratch_shapes=[
                pltpu.VMEM((count * PIECE, columns), jnp.bfloat16),
                pltpu.SemaphoreType.DMA((count,)),
            ],
        ),
        out_shape=[jax.ShapeDtypeStruct((answers, wide), jnp.float32)] * CHIPS,
        compiler_params=pltpu.CompilerParams(vmem_limit_bytes=48 * 2**20),
        cost_estimate=pl.CostEstimate(
            flops=flops,
            bytes_accessed=questions * rows * (8 * columns + 4 * count * PIECE),
            transcendentals=questions * rows * answers * columns // HD,
        ),
        name="attend",
    )(info, *([own_rows] * count), *([other_rows] * count), before, queries, live, *arrays)


def merge_kernel(*refs):
    parts, out = refs[:-1], refs[-1]
    answers, width = out.shape
    heads = width // HD
    lane = lax.broadcasted_iota(jnp.int32, (answers, 128), 1)
    tails = [part[:, pl.ds(width, 128)] for part in parts]
    peak = functools.reduce(jnp.maximum, tails)
    factors = [jnp.exp(jnp.where(lane < heads, tail - peak, 0.0)) for tail in tails]

    def column(value, at):
        return value[:, at : at + 1]

    for tile in range(width // 128):
        low, high = 2 * tile, 2 * tile + 1
        numer = jnp.zeros((answers, 128), jnp.float32)
        total = jnp.zeros((answers, 128), jnp.float32)
        for part, tail, factor in zip(parts, tails, factors):
            scale = jnp.where(lane < HD, column(factor, low), column(factor, high))
            amount = jnp.where(lane < HD, column(tail, heads + low), column(tail, heads + high))
            numer += part[:, pl.ds(tile * 128, 128)] * scale
            total += amount * scale
        out[:, pl.ds(tile * 128, 128)] = (numer / total).astype(out.dtype)


def merge(parts):
    answers, wide = parts[0].shape
    return pl.pallas_call(
        merge_kernel,
        out_shape=jax.ShapeDtypeStruct((answers, wide - 128), jnp.bfloat16),
        cost_estimate=pl.CostEstimate(flops=8 * answers * wide, bytes_accessed=16 * answers * wide, transcendentals=512 * answers),
        name="merge",
    )(*parts)


def gathered_shards(
    decoder_states,
    norm_gain,
    query_weight,
    key_weight,
    value_weight,
    out_weight,
    passage_states,
    block_mask,
):
    pb_index = lax.axis_index("pb")
    f = lax.axis_index("fsdp")
    z, c = pb_index // 2, pb_index % 2
    questions, rows, model_width = passage_states.shape
    width = key_weight.shape[1] // 2

    def core_columns(core):
        return jnp.concatenate(
            [lax.dynamic_slice_in_dim(w, core * width, width, 1) for w in (key_weight, value_weight)], axis=1
        )

    own = core_columns(c)
    partner = core_swap(core_columns(1 - c))
    early, later, last = gather_pieces(own, partner, z)
    other_rows = core_swap(after((passage_states,), (partner,))[0])

    own_states = decoder_states[0]
    states_wide = own_states.astype(jnp.float32)
    square_part = jnp.sum(states_wide * states_wide, axis=1, keepdims=True)
    scaled = (states_wide * norm_gain.astype(jnp.float32)[None, :]).astype(jnp.bfloat16)
    query_part = jnp.dot(scaled, query_weight, preferred_element_type=jnp.float32)
    both = jnp.concatenate([query_part, jnp.broadcast_to(square_part, (square_part.shape[0], 128))], axis=1)
    both = both + lax.ppermute(both, "fsdp", [(0, 1), (1, 0)])
    query_raw, square_sum = both[:, :-128], both[:, -128:-127]
    query = (query_raw * lax.rsqrt(square_sum / model_width + 1e-06)).astype(jnp.bfloat16)
    every_query = lax.all_gather(query, "pb")
    queries = lax.dynamic_slice(
        every_query, (f * questions, 0, c * width), (questions, query.shape[0], width)
    )

    blocks_here = rows // BLOCK
    mine = lax.dynamic_slice_in_dim(block_mask, f * questions, questions, 0)
    live = jnp.concatenate(
        [lax.dynamic_slice_in_dim(mine, p * blocks_here, blocks_here, 1) for p in (pb_index, pb_index ^ 1)],
        axis=1,
    )
    live = jnp.repeat(live, BLOCK, axis=1)[:, None, :]

    def info(pieces):
        return jnp.concatenate([z[None], feature_blocks(pieces, z, c, f)]).astype(jnp.int32)

    sums = project_pieces(info(early), early, passage_states, other_rows)
    sums = project_pieces(info(later), later, passage_states, other_rows, sums)
    parts = attend_last(info(last), last, passage_states, other_rows, sums, queries, live)
    arrived = [parts[0]]
    for step in range(1, CHIPS):
        turn = [(2 * k + core, 2 * ((k + step) % CHIPS) + core) for k in range(CHIPS) for core in range(2)]
        arrived.append(lax.ppermute(parts[step], "pb", turn))
    attention = merge(arrived)

    received = []
    for flip in range(2):
        sends = [
            (2 * (2 * k + core) + x, 2 * (questions * x + k) + (core ^ flip))
            for k in range(CHIPS)
            for core in range(2)
            for x in range(2)
        ]
        received.append(lax.ppermute(attention, ("pb", "fsdp"), sends))
    first = jnp.where(f == 0, received[0], received[1])
    second = jnp.where(f == 0, received[1], received[0])
    whole = jnp.concatenate([first, second], axis=1)
    partial_out = jnp.dot(whole, out_weight, preferred_element_type=jnp.float32).astype(jnp.bfloat16)
    other_out = lax.ppermute(partial_out, "section", [(0, 1), (1, 0)])
    summed = (partial_out.astype(jnp.float32) + other_out.astype(jnp.float32)).astype(jnp.bfloat16)
    return summed[None]


def solution(mesh):
    placed = (
        P("pb", None, "fsdp"),
        P("fsdp"),
        P("fsdp", "section"),
        P(("pb", "fsdp"), "section"),
        P(("pb", "fsdp"), "section"),
        P("section", "fsdp"),
        P("fsdp", "pb", None),
        P(),
    )
    sizes = dict(mesh.shape)
    fits = sizes == {"section": 2, "pb": 2 * CHIPS, "fsdp": 2}
    return jax.shard_map(
        gathered_shards if fits else plain_shards,
        mesh=mesh,
        in_specs=placed,
        out_specs=P("pb", None, "fsdp"),
        check_vma=False,
    )
```

```python
import functools

import jax
import jax.numpy as jnp
from jax import lax
from jax.experimental import pallas as pl
from jax.experimental.pallas import tpu as pltpu
from jax.sharding import PartitionSpec as P

HD = 64
BLOCK = 128
PASSAGE = 256


NEGATIVE = -1e30


def joined(value, axis, combine):
    everything = jax.tree.map(lambda part: lax.all_gather(part, axis), value)
    leading = jax.tree.map(lambda part: part[0], everything)

    def turn(k, so_far):
        return combine(so_far, jax.tree.map(lambda part: part[k], everything))

    return lax.fori_loop(1, lax.axis_size(axis), turn, leading)


def pack_order(alive_flags):
    amount = alive_flags.shape[0]
    ahead_count = jnp.cumsum(alive_flags) - alive_flags
    behind = jnp.cumsum(1 - alive_flags) - (1 - alive_flags)
    filled = jnp.sum(alive_flags)
    slot_index = jnp.where(alive_flags > 0, ahead_count, filled + behind)
    places = jnp.arange(amount, dtype=jnp.int32)
    order_index = jnp.sum(
        jnp.where(slot_index[None, :] == places[:, None], places[None, :], 0), axis=1
    )
    return (slot_index, order_index, filled)


def project(pieces, alive_flags, stacked):
    amount, piece_rows, model_width = pieces.shape
    slot_index, order_index, filled = pack_order(alive_flags)
    packed = pieces[order_index]
    per_group = min(amount, max(1, 256 // piece_rows))
    columns = stacked.shape[1]

    def compute(row_block):
        return jnp.dot(row_block, stacked, preferred_element_type=jnp.float32).astype(jnp.bfloat16)

    def skipped(row_block):
        return jnp.zeros((row_block.shape[0], columns), jnp.bfloat16)

    def advance(group_index, buffer):
        first_piece = group_index * per_group
        row_block = lax.dynamic_slice_in_dim(packed, first_piece, per_group, 0).reshape(
            per_group * piece_rows, model_width
        )
        result = lax.cond(first_piece < filled, compute, skipped, row_block)
        return lax.dynamic_update_slice_in_dim(
            buffer, result.reshape(per_group, piece_rows, columns), first_piece, 0
        )

    empty_buffer = jnp.zeros((amount, piece_rows, columns), jnp.bfloat16)
    buffer = lax.fori_loop(0, amount // per_group, advance, empty_buffer)
    return (buffer, slot_index, filled)


def attend(query, keyval, live_rows):
    row_total, doubled = keyval.shape
    half_width = doubled // 2
    head_count = half_width // HD
    answer_len = query.shape[0]
    keys_part = keyval[:, :half_width].reshape(row_total, head_count, HD)
    values_part = keyval[:, half_width:].reshape(row_total, head_count, HD)
    queries = query.reshape(answer_len, head_count, HD)
    scores = jnp.einsum("ahd,rhd->ahr", queries, keys_part, preferred_element_type=jnp.float32)
    shown = live_rows[None, None, :]
    scores = jnp.where(shown, scores, NEGATIVE)
    peak = jnp.max(scores, axis=2)
    raw_weights = jnp.where(shown, jnp.exp(scores - peak[:, :, None]), 0.0)
    totals = jnp.sum(raw_weights, axis=2)
    numerator = jnp.einsum(
        "ahr,rhd->ahd",
        raw_weights.astype(jnp.bfloat16),
        values_part,
        preferred_element_type=jnp.float32,
    )
    return (peak, totals, numerator)


def combine_parts(first, second):
    peak_one, totals_one, numer_one = first
    peak_two, totals_two, numer_two = second
    peak = jnp.maximum(peak_one, peak_two)
    factor_one = jnp.exp(peak_one - peak)
    factor_two = jnp.exp(peak_two - peak)
    totals = totals_one * factor_one + totals_two * factor_two
    numerator = numer_one * factor_one[:, :, None] + numer_two * factor_two[:, :, None]
    return (peak, totals, numerator)


def plain_shards(
    decoder_states,
    norm_gain,
    query_weight,
    key_weight,
    value_weight,
    out_weight,
    passage_states,
    block_mask,
):
    pb_count = lax.axis_size("pb")
    fsdp_count = lax.axis_size("fsdp")
    pb_index = lax.axis_index("pb")
    fsdp_index = lax.axis_index("fsdp")
    local_questions, local_rows, model_width = passage_states.shape
    block_total = block_mask.shape[1]
    passages_here = local_rows // PASSAGE
    piece_rows = PASSAGE // fsdp_count
    block_ids = jnp.arange(block_total, dtype=jnp.int32)
    own_mask = lax.dynamic_slice_in_dim(block_mask, pb_index, 1, 0)[0]
    passage_ids = jnp.arange(pb_count * passages_here, dtype=jnp.int32)
    piece_block = (passage_ids * PASSAGE + fsdp_index * piece_rows) // BLOCK
    decoder_live = jnp.sum(
        jnp.where(piece_block[:, None] == block_ids[None, :], own_mask[None, :], 0), axis=1
    )
    stacked_local = jnp.concatenate([key_weight, value_weight], axis=1)
    stacked = lax.all_gather(stacked_local, ("pb", "fsdp"), axis=0, tiled=True)
    own_states = decoder_states[0]
    states_wide = own_states.astype(jnp.float32)
    square_part = jnp.sum(states_wide * states_wide, axis=1)
    scaled = (states_wide * norm_gain.astype(jnp.float32)[None, :]).astype(jnp.bfloat16)
    query_part = jnp.dot(scaled, query_weight, preferred_element_type=jnp.float32)
    square_sum, query_raw = lax.psum((square_part, query_part), "fsdp")
    query = (query_raw * lax.rsqrt(square_sum / model_width + 1e-06)[:, None]).astype(jnp.bfloat16)
    shaped = passage_states.reshape(
        local_questions, passages_here, fsdp_count, piece_rows, model_width
    )
    by_piece = lax.all_to_all(shaped, "fsdp", split_axis=2, concat_axis=0, tiled=True)
    by_question = lax.all_to_all(by_piece, "pb", split_axis=0, concat_axis=1, tiled=True)
    pieces = by_question.reshape(pb_count * passages_here, piece_rows, model_width)
    projected, slot_index, filled = project(pieces, decoder_live, stacked)
    keyval = projected.reshape(pb_count * passages_here * piece_rows, projected.shape[2])
    live_rows = jnp.repeat(passage_ids < filled, piece_rows)
    peak, totals, numerator = attend(query, keyval, live_rows)
    peak, totals, numerator = joined((peak, totals, numerator), "fsdp", combine_parts)
    attention = (
        (numerator / totals[:, :, None])
        .astype(jnp.bfloat16)
        .reshape(query.shape[0], query.shape[1])
    )
    partial_out = jnp.dot(attention, out_weight, preferred_element_type=jnp.float32)
    summed_out = lax.psum(partial_out.astype(jnp.bfloat16), "section")
    return summed_out[None]


CHIPS = 4
VMEM_LIMIT = 56 * 2**20
PIECE = 256


def line(step, sources):
    return [(2 * z + c, 2 * (z + step) + c) for z in sources for c in range(2)]


def nothing(*refs):
    pass


def after(values, done):
    anywhere = pl.BlockSpec(memory_space=pl.ANY)
    count = len(values)
    return pl.pallas_call(
        nothing,
        in_specs=[anywhere] * (count + len(done)),
        out_specs=[anywhere] * count,
        out_shape=[jax.ShapeDtypeStruct(value.shape, value.dtype) for value in values],
        input_output_aliases={k: k for k in range(count)},
        name="after",
    )(*values, *done)


def by_chip(z, options):
    picked = options[0]
    for place in range(1, CHIPS):
        if options[place] is not picked:
            picked = jnp.where(z >= place, options[place], picked)
    return picked


def core_swap(value):
    return lax.ppermute(value, "pb", [(p, p ^ 1) for p in range(2 * CHIPS)])


def gather_pieces(own, partner, z, add_pieces, terms, pair_of, questions, other_rows):
    def left(value, sources):
        return lax.ppermute(value, "pb", line(-1, sources))

    def right(value, sources):
        return lax.ppermute(value, "pb", line(1, sources))

    def outward(value):
        return lax.ppermute(value, "pb", line(-1, (1,)) + line(1, (2,)))

    def across(value):
        return lax.ppermute(value, "fsdp", [(0, 1), (1, 0)])

    here, second, third, fourth = (0, 1, 2, 3), (1, 2, 1, 2), (2, 0, 3, 1), (3, 3, 0, 0)

    x_b = across(own)
    l_b1, r_b1 = left(own, (1, 2, 3)), right(own, (0, 1, 2))
    l_a1, r_a1 = left(partner, (1, 2, 3)), right(partner, (0, 1, 2))
    x_a = across(partner)

    both = terms + across(terms)
    pair = pair_of(both)

    l_b2 = left(jnp.where(z == 3, x_b, l_b1), (1, 2, 3))
    r_b2 = right(jnp.where(z == 0, x_b, r_b1), (0, 1, 2))
    l_a2, r_a2 = left(l_a1, (1, 2)), right(r_a1, (1, 2))
    ab1 = jnp.where(z < 2, jnp.concatenate([l_a1, l_b1]), jnp.concatenate([r_a1, r_b1]))
    (ab1,) = after((ab1,), (x_a,))
    x_ab1 = across(ab1)

    l_b3, r_b3 = left(l_b2, (1, 2)), right(r_b2, (1, 2))
    end_a3 = outward(jnp.where(z < 2, l_a2, r_a2))
    a2 = by_chip(z, (l_a2, r_a1, l_a1, r_a2))
    ab2 = jnp.concatenate([a2, jnp.where(z < 2, l_b2, r_b2)])
    x_ab2 = across(ab2)

    def all_z(piece, part=0):
        return ((piece, part),) * 4

    def each_z(*pieces):
        return tuple((piece, 0) for piece in pieces)

    sums, token = add_pieces(
        [
            (all_z(own), here, 0, 0),
            (all_z(partner), here, 0, 1),
            (all_z(x_b), here, 1, 0),
            (all_z(x_a), here, 1, 1),
            (all_z(ab1, 0), second, 0, 1),
            (all_z(ab1, 1), second, 0, 0),
            (all_z(x_ab1, 0), second, 1, 1),
            (all_z(x_ab1, 1), second, 1, 0),
            (all_z(ab2, 0), third, 0, 1),
            (each_z(l_b2, r_b1, l_b1, r_b2), third, 0, 0),
        ],
        None,
    )

    end_a3, l_b3, r_b3 = after((end_a3, l_b3, r_b3), (token,))
    a3 = by_chip(z, (end_a3, l_a2, r_a2, end_a3))
    x_a3 = across(a3)
    end_b4 = outward(jnp.where(z < 2, l_b3, r_b3))
    queries = spread_queries(after((pair,), (token,))[0], questions)

    sums, token = add_pieces(
        [
            (all_z(a3), fourth, 0, 1),
            (each_z(l_b3, l_b2, r_b2, r_b3), fourth, 0, 0),
            (all_z(x_ab2, 0), third, 1, 1),
            (((x_ab2, 1), (r_b2, 0), (l_b2, 0), (x_ab2, 1)), third, 1, 0),
        ],
        sums,
    )
    last = [
        (all_z(x_a3), fourth, 1, 1),
        (each_z(end_b4, l_b3, r_b3, end_b4), fourth, 1, 0),
    ]
    return sums, last, queries


def feature_blocks(pieces, z, c, f):
    found = []
    for _, origins, other_x, other_core in pieces:
        origin = by_chip(z, [jnp.int32(o) for o in origins])
        core = 1 - c if other_core else c
        place = 1 - f if other_x else f
        found.append(4 * origin + 2 * core + place)
    return jnp.stack(found)


def distinct(pieces):
    arrays, wanted = [], []
    for options, _, _, _ in pieces:
        spots = []
        for option, part in options:
            at = next((k for k, seen in enumerate(arrays) if seen is option), None)
            if at is None:
                at = len(arrays)
                arrays.append(option)
            spots.append((at, part))
        wanted.append(spots)
    return arrays, wanted


def load_weights(wanted, z, sources, weights, sems):
    def copy(slot, spot):
        at, part = spot
        return pltpu.make_async_copy(
            sources[at].at[pl.ds(part * PIECE, PIECE)], weights.at[pl.ds(slot * PIECE, PIECE)], sems.at[slot]
        )

    for slot, spots in enumerate(wanted):
        for spot in sorted(set(spots)):
            zs = [k for k, other in enumerate(spots) if other == spot]
            begin = copy(slot, spot).start
            if len(zs) == CHIPS:
                begin()
            else:
                pl.when(functools.reduce(jnp.logical_or, [z == k for k in zs]))(lambda begin=begin: begin())
    for slot, spots in enumerate(wanted):
        copy(slot, spots[0]).wait()


def project_kernel(wanted, amount, carried, info, *refs):
    refs = list(refs)
    count = len(wanted)
    halves, refs = (refs[:count], refs[count : 2 * count]), refs[2 * count :]
    before = refs.pop(0) if carried else None
    sources, (total, token, weights, sems) = refs[:amount], refs[amount:]

    question = pl.program_id(0)

    @pl.when(question == 0)
    def _():
        load_weights(wanted, info[0], sources, weights, sems)
        token[...] = jnp.zeros_like(token)

    for half, blocks in enumerate(halves):
        rows = blocks[0].shape[1]
        here = pl.ds(half * rows, rows)
        features = jnp.concatenate([block[0] for block in blocks], axis=1)
        part = jnp.dot(features, weights[...], preferred_element_type=jnp.float32)
        if carried:
            part = part + before[0, here, :]
        total[0, here, :] = part


def project_pieces(info, pieces, own_rows, other_rows, before=None):
    questions, rows, width = own_rows.shape
    columns = pieces[0][0][0][0].shape[1]
    arrays, wanted = distinct(pieces)
    count = len(pieces)
    carried = before is not None
    blocks = [pl.BlockSpec((1, rows, PIECE), lambda i, info, k=k: (i, 0, info[1 + k])) for k in range(count)]
    sums = pl.BlockSpec((1, 2 * rows, columns), lambda i, info: (i, 0, 0))
    anywhere = pl.BlockSpec(memory_space=pl.ANY)
    return pl.pallas_call(
        functools.partial(project_kernel, wanted, len(arrays), carried),
        grid_spec=pltpu.PrefetchScalarGridSpec(
            num_scalar_prefetch=1,
            grid=(questions,),
            in_specs=blocks + blocks + ([sums] if carried else []) + [anywhere] * len(arrays),
            out_specs=[sums, pl.BlockSpec((8, 128), lambda i, info: (0, 0))],
            scratch_shapes=[
                pltpu.VMEM((count * PIECE, columns), jnp.bfloat16),
                pltpu.SemaphoreType.DMA((count,)),
            ],
        ),
        out_shape=[
            jax.ShapeDtypeStruct((questions, 2 * rows, columns), jnp.float32),
            jax.ShapeDtypeStruct((8, 128), jnp.float32),
        ],
        input_output_aliases={2 * count + 1: 0} if carried else {},
        compiler_params=pltpu.CompilerParams(vmem_limit_bytes=VMEM_LIMIT),
        cost_estimate=pl.CostEstimate(flops=1000, bytes_accessed=1000, transcendentals=0),
        name="project",
    )(info, *([own_rows] * count), *([other_rows] * count), *([before] if carried else []), *arrays)


def attend_kernel(wanted, amount, info, *refs):
    refs = list(refs)
    count = len(wanted)
    halves, refs = (refs[:count], refs[count : 2 * count]), refs[2 * count :]
    before, queries, live, refs = refs[0], refs[1], refs[2], refs[3:]
    sources, refs = refs[:amount], refs[amount:]
    outs, (weights, sems) = refs[:CHIPS], refs[CHIPS:]
    step = pl.program_id(0)

    @pl.when(step == 0)
    def _():
        load_weights(wanted, info[0], sources, weights, sems)

    found = []
    for half, blocks in enumerate(halves):
        rows = blocks[0].shape[1]
        features = jnp.concatenate([block[0] for block in blocks], axis=1)
        part = jnp.dot(features, weights[...], preferred_element_type=jnp.float32)
        found.append((part + before[0, pl.ds(half * rows, rows), :]).astype(jnp.bfloat16))
    keyval = jnp.concatenate(found, axis=0)
    width = keyval.shape[1] // 2
    answers = queries.shape[1]
    group = 4
    span = group * HD
    shown = live[0] > 0
    lane_head = lax.broadcasted_iota(jnp.int32, (answers, span), 1) // HD
    tail_lane = lax.broadcasted_iota(jnp.int32, (answers, 128), 1)
    head_total = width // HD
    extra = jnp.zeros((answers, 128), jnp.float32)
    parts = []
    for g in range(width // span):
        at = slice(g * span, (g + 1) * span)
        query = queries[0, :, at]
        spread = jnp.concatenate(
            [jnp.where(lane_head == h, query, jnp.zeros_like(query)) for h in range(group)], axis=0
        )
        scores = lax.dot_general(
            spread, keyval[:, at], (((1,), (1,)), ((), ())), preferred_element_type=jnp.float32
        )
        scores = jnp.where(shown, scores, NEGATIVE)
        peak = jnp.max(scores, axis=1, keepdims=True)
        raw = jnp.where(shown, jnp.exp(scores - peak), 0.0)
        total = jnp.sum(raw, axis=1, keepdims=True)
        value_at = slice(width + g * span, width + (g + 1) * span)
        numer = jnp.dot(raw.astype(jnp.bfloat16), keyval[:, value_at], preferred_element_type=jnp.float32)
        own = jnp.zeros((answers, span), jnp.float32)
        for h in range(group):
            mine = slice(h * answers, (h + 1) * answers)
            own = jnp.where(lane_head == h, numer[mine], own)
            extra = jnp.where(tail_lane == g * group + h, peak[mine], extra)
            extra = jnp.where(tail_lane == head_total + g * group + h, total[mine], extra)
        parts.append(own)
    result = jnp.concatenate(parts + [extra], axis=1)
    for k, out in enumerate(outs):

        @pl.when(step == k)
        def _(out=out):
            out[...] = result


def attend_last(info, pieces, own_rows, other_rows, before, queries, live):
    questions, rows, width = own_rows.shape
    columns = pieces[0][0][0][0].shape[1]
    answers = queries.shape[1]
    arrays, wanted = distinct(pieces)
    count = len(pieces)
    wide = columns // 2 + 128

    def question(i, info):
        return lax.rem(i + info[0], questions)

    def turned(i, info):
        wanted = question(i, info)
        pairs = questions // 2
        return 2 * lax.rem(wanted // 2 + info[0] * (pairs - 1), pairs) + lax.rem(wanted, 2)


    blocks = [
        pl.BlockSpec((1, rows, PIECE), lambda i, info, k=k: (question(i, info), 0, info[1 + k]))
        for k in range(count)
    ]
    whole = lambda *shape: pl.BlockSpec((1,) + shape, lambda i, info: (question(i, info), 0, 0))
    anywhere = pl.BlockSpec(memory_space=pl.ANY)
    flops = 4 * questions * rows * count * PIECE * columns + 16 * questions * rows * answers * columns
    return pl.pallas_call(
        functools.partial(attend_kernel, wanted, len(arrays)),
        grid_spec=pltpu.PrefetchScalarGridSpec(
            num_scalar_prefetch=1,
            grid=(questions,),
            in_specs=blocks
            + blocks
            + [
                whole(2 * rows, columns),
                pl.BlockSpec((1, answers, columns // 2), lambda i, info: (turned(i, info), 0, 0)),
                whole(1, 2 * rows),
            ]
            + [anywhere] * len(arrays),
            out_specs=[pl.BlockSpec((answers, wide), lambda i, info: (0, 0))] * CHIPS,
            scratch_shapes=[
                pltpu.VMEM((count * PIECE, columns), jnp.bfloat16),
                pltpu.SemaphoreType.DMA((count,)),
            ],
        ),
        out_shape=[jax.ShapeDtypeStruct((answers, wide), jnp.float32)] * CHIPS,
        compiler_params=pltpu.CompilerParams(vmem_limit_bytes=VMEM_LIMIT),
        cost_estimate=pl.CostEstimate(
            flops=flops,
            bytes_accessed=questions * rows * (8 * columns + 4 * count * PIECE),
            transcendentals=questions * rows * answers * columns // HD,
        ),
        name="attend",
    )(info, *([own_rows] * count), *([other_rows] * count), before, queries, live, *arrays)


def merge_kernel(*refs):
    parts, out = refs[:-1], refs[-1]
    answers, width = out.shape
    heads = width // HD
    lane = lax.broadcasted_iota(jnp.int32, (answers, 128), 1)
    tails = [part[:, pl.ds(width, 128)] for part in parts]
    peak = functools.reduce(jnp.maximum, tails)
    factors = [jnp.exp(jnp.where(lane < heads, tail - peak, 0.0)) for tail in tails]

    def column(value, at):
        return value[:, at : at + 1]

    for tile in range(width // 128):
        low, high = 2 * tile, 2 * tile + 1
        numer = jnp.zeros((answers, 128), jnp.float32)
        total = jnp.zeros((answers, 128), jnp.float32)
        for part, tail, factor in zip(parts, tails, factors):
            scale = jnp.where(lane < HD, column(factor, low), column(factor, high))
            amount = jnp.where(lane < HD, column(tail, heads + low), column(tail, heads + high))
            numer += part[:, pl.ds(tile * 128, 128)] * scale
            total += amount * scale
        out[:, pl.ds(tile * 128, 128)] = (numer / total).astype(out.dtype)


def merge(parts):
    answers, wide = parts[0].shape
    return pl.pallas_call(
        merge_kernel,
        out_shape=jax.ShapeDtypeStruct((answers, wide - 128), jnp.bfloat16),
        cost_estimate=pl.CostEstimate(flops=8 * answers * wide, bytes_accessed=16 * answers * wide, transcendentals=512 * answers),
        name="merge",
    )(*parts)


def query_terms(states, norm_gain, query_weight):
    states_wide = states.astype(jnp.float32)
    square_part = jnp.sum(states_wide * states_wide, axis=1, keepdims=True)
    scaled = (states_wide * norm_gain.astype(jnp.float32)[None, :]).astype(jnp.bfloat16)
    query_part = jnp.dot(scaled, query_weight, preferred_element_type=jnp.float32)
    return jnp.concatenate([query_part, jnp.broadcast_to(square_part, (square_part.shape[0], 128))], axis=1)


def spread_queries(pair, questions):
    pairs = questions // 2
    spread = []
    for turn in range(pairs):
        sends = []
        for place in range(2):
            for to in range(CHIPS):
                chip = pairs * place + (to + turn) % pairs
                for core in range(2):
                    sends.append((2 * (2 * chip + core) + to // pairs, 2 * (2 * to + core) + place))
        spread.append(lax.ppermute(pair, ("pb", "fsdp"), sends))
    return spread


def gathered_shards(
    decoder_states,
    norm_gain,
    query_weight,
    key_weight,
    value_weight,
    out_weight,
    passage_states,
    block_mask,
):
    pb_index = lax.axis_index("pb")
    f = lax.axis_index("fsdp")
    z, c = pb_index // 2, pb_index % 2
    questions, rows, model_width = passage_states.shape
    width = key_weight.shape[1] // 2

    def core_columns(core):
        return jnp.concatenate(
            [lax.dynamic_slice_in_dim(w, core * width, width, 1) for w in (key_weight, value_weight)], axis=1
        )

    own = core_columns(c)
    partner = core_swap(core_columns(1 - c))
    other_rows = core_swap(passage_states)

    def info(pieces):
        return jnp.concatenate([z[None], feature_blocks(pieces, z, c, f)]).astype(jnp.int32)

    def add_pieces(pieces, sums):
        return project_pieces(info(pieces), pieces, passage_states, other_rows, sums)

    terms = query_terms(decoder_states[0], norm_gain, query_weight)

    def pair_of(both):
        query_raw, square_sum = both[:, :-128], both[:, -128:-127]
        query = (query_raw * lax.rsqrt(square_sum / model_width + 1e-06)).astype(jnp.bfloat16)
        mine = lax.dynamic_slice_in_dim(query, c * width, width, 1)
        theirs = core_swap(lax.dynamic_slice_in_dim(query, (1 - c) * width, width, 1))
        return jnp.stack([jnp.where(c == 0, mine, theirs), jnp.where(c == 0, theirs, mine)])

    sums, last, queries = gather_pieces(own, partner, z, add_pieces, terms, pair_of, questions, other_rows)
    queries = jnp.concatenate(queries, axis=0)

    blocks_here = rows // BLOCK
    mine = lax.dynamic_slice_in_dim(block_mask, f * questions, questions, 0)
    live = jnp.concatenate(
        [lax.dynamic_slice_in_dim(mine, p * blocks_here, blocks_here, 1) for p in (pb_index, pb_index ^ 1)],
        axis=1,
    )
    live = jnp.repeat(live, BLOCK, axis=1)[:, None, :]

    parts = attend_last(info(last), last, passage_states, other_rows, sums, queries, live)
    arrived = [parts[0]]
    for step in range(1, CHIPS):
        turn = [(2 * k + core, 2 * ((k + step) % CHIPS) + core) for k in range(CHIPS) for core in range(2)]
        arrived.append(lax.ppermute(parts[step], "pb", turn))
    attention = merge(arrived)

    received = []
    for flip in range(2):
        sends = [
            (2 * (2 * k + core) + x, 2 * (questions * x + k) + (core ^ flip))
            for k in range(CHIPS)
            for core in range(2)
            for x in range(2)
        ]
        received.append(lax.ppermute(attention, ("pb", "fsdp"), sends))
    first = jnp.where(f == 0, received[0], received[1])
    second = jnp.where(f == 0, received[1], received[0])
    whole = jnp.concatenate([first, second], axis=1)
    partial_out = jnp.dot(whole, out_weight, preferred_element_type=jnp.float32).astype(jnp.bfloat16)
    other_out = lax.ppermute(partial_out, "section", [(0, 1), (1, 0)])
    summed = (partial_out.astype(jnp.float32) + other_out.astype(jnp.float32)).astype(jnp.bfloat16)
    return summed[None]


def solution(mesh):
    placed = (
        P("pb", None, "fsdp"),
        P("fsdp"),
        P("fsdp", "section"),
        P(("pb", "fsdp"), "section"),
        P(("pb", "fsdp"), "section"),
        P("section", "fsdp"),
        P("fsdp", "pb", None),
        P(),
    )
    sizes = dict(mesh.shape)
    fits = sizes == {"section": 2, "pb": 2 * CHIPS, "fsdp": 2}
    return jax.shard_map(
        gathered_shards if fits else plain_shards,
        mesh=mesh,
        in_specs=placed,
        out_specs=P("pb", None, "fsdp"),
        check_vma=False,
    )
```

```python
import functools

import jax
import jax.numpy as jnp
from jax import lax
from jax.experimental import pallas as pl
from jax.experimental.pallas import tpu as pltpu
from jax.sharding import PartitionSpec as P

HD = 64
BLOCK = 128
PASSAGE = 256


NEGATIVE = -1e30


def joined(value, axis, combine):
    everything = jax.tree.map(lambda part: lax.all_gather(part, axis), value)
    leading = jax.tree.map(lambda part: part[0], everything)

    def turn(k, so_far):
        return combine(so_far, jax.tree.map(lambda part: part[k], everything))

    return lax.fori_loop(1, lax.axis_size(axis), turn, leading)


def pack_order(alive_flags):
    amount = alive_flags.shape[0]
    ahead_count = jnp.cumsum(alive_flags) - alive_flags
    behind = jnp.cumsum(1 - alive_flags) - (1 - alive_flags)
    filled = jnp.sum(alive_flags)
    slot_index = jnp.where(alive_flags > 0, ahead_count, filled + behind)
    places = jnp.arange(amount, dtype=jnp.int32)
    order_index = jnp.sum(
        jnp.where(slot_index[None, :] == places[:, None], places[None, :], 0), axis=1
    )
    return (slot_index, order_index, filled)


def project(pieces, alive_flags, stacked):
    amount, piece_rows, model_width = pieces.shape
    slot_index, order_index, filled = pack_order(alive_flags)
    packed = pieces[order_index]
    per_group = min(amount, max(1, 256 // piece_rows))
    columns = stacked.shape[1]

    def compute(row_block):
        return jnp.dot(row_block, stacked, preferred_element_type=jnp.float32).astype(jnp.bfloat16)

    def skipped(row_block):
        return jnp.zeros((row_block.shape[0], columns), jnp.bfloat16)

    def advance(group_index, buffer):
        first_piece = group_index * per_group
        row_block = lax.dynamic_slice_in_dim(packed, first_piece, per_group, 0).reshape(
            per_group * piece_rows, model_width
        )
        result = lax.cond(first_piece < filled, compute, skipped, row_block)
        return lax.dynamic_update_slice_in_dim(
            buffer, result.reshape(per_group, piece_rows, columns), first_piece, 0
        )

    empty_buffer = jnp.zeros((amount, piece_rows, columns), jnp.bfloat16)
    buffer = lax.fori_loop(0, amount // per_group, advance, empty_buffer)
    return (buffer, slot_index, filled)


def attend(query, keyval, live_rows):
    row_total, doubled = keyval.shape
    half_width = doubled // 2
    head_count = half_width // HD
    answer_len = query.shape[0]
    keys_part = keyval[:, :half_width].reshape(row_total, head_count, HD)
    values_part = keyval[:, half_width:].reshape(row_total, head_count, HD)
    queries = query.reshape(answer_len, head_count, HD)
    scores = jnp.einsum("ahd,rhd->ahr", queries, keys_part, preferred_element_type=jnp.float32)
    shown = live_rows[None, None, :]
    scores = jnp.where(shown, scores, NEGATIVE)
    peak = jnp.max(scores, axis=2)
    raw_weights = jnp.where(shown, jnp.exp(scores - peak[:, :, None]), 0.0)
    totals = jnp.sum(raw_weights, axis=2)
    numerator = jnp.einsum(
        "ahr,rhd->ahd",
        raw_weights.astype(jnp.bfloat16),
        values_part,
        preferred_element_type=jnp.float32,
    )
    return (peak, totals, numerator)


def combine_parts(first, second):
    peak_one, totals_one, numer_one = first
    peak_two, totals_two, numer_two = second
    peak = jnp.maximum(peak_one, peak_two)
    factor_one = jnp.exp(peak_one - peak)
    factor_two = jnp.exp(peak_two - peak)
    totals = totals_one * factor_one + totals_two * factor_two
    numerator = numer_one * factor_one[:, :, None] + numer_two * factor_two[:, :, None]
    return (peak, totals, numerator)


def plain_shards(
    decoder_states,
    norm_gain,
    query_weight,
    key_weight,
    value_weight,
    out_weight,
    passage_states,
    block_mask,
):
    pb_count = lax.axis_size("pb")
    fsdp_count = lax.axis_size("fsdp")
    pb_index = lax.axis_index("pb")
    fsdp_index = lax.axis_index("fsdp")
    local_questions, local_rows, model_width = passage_states.shape
    block_total = block_mask.shape[1]
    passages_here = local_rows // PASSAGE
    piece_rows = PASSAGE // fsdp_count
    block_ids = jnp.arange(block_total, dtype=jnp.int32)
    own_mask = lax.dynamic_slice_in_dim(block_mask, pb_index, 1, 0)[0]
    passage_ids = jnp.arange(pb_count * passages_here, dtype=jnp.int32)
    piece_block = (passage_ids * PASSAGE + fsdp_index * piece_rows) // BLOCK
    decoder_live = jnp.sum(
        jnp.where(piece_block[:, None] == block_ids[None, :], own_mask[None, :], 0), axis=1
    )
    stacked_local = jnp.concatenate([key_weight, value_weight], axis=1)
    stacked = lax.all_gather(stacked_local, ("pb", "fsdp"), axis=0, tiled=True)
    own_states = decoder_states[0]
    states_wide = own_states.astype(jnp.float32)
    square_part = jnp.sum(states_wide * states_wide, axis=1)
    scaled = (states_wide * norm_gain.astype(jnp.float32)[None, :]).astype(jnp.bfloat16)
    query_part = jnp.dot(scaled, query_weight, preferred_element_type=jnp.float32)
    square_sum, query_raw = lax.psum((square_part, query_part), "fsdp")
    query = (query_raw * lax.rsqrt(square_sum / model_width + 1e-06)[:, None]).astype(jnp.bfloat16)
    shaped = passage_states.reshape(
        local_questions, passages_here, fsdp_count, piece_rows, model_width
    )
    by_piece = lax.all_to_all(shaped, "fsdp", split_axis=2, concat_axis=0, tiled=True)
    by_question = lax.all_to_all(by_piece, "pb", split_axis=0, concat_axis=1, tiled=True)
    pieces = by_question.reshape(pb_count * passages_here, piece_rows, model_width)
    projected, slot_index, filled = project(pieces, decoder_live, stacked)
    keyval = projected.reshape(pb_count * passages_here * piece_rows, projected.shape[2])
    live_rows = jnp.repeat(passage_ids < filled, piece_rows)
    peak, totals, numerator = attend(query, keyval, live_rows)
    peak, totals, numerator = joined((peak, totals, numerator), "fsdp", combine_parts)
    attention = (
        (numerator / totals[:, :, None])
        .astype(jnp.bfloat16)
        .reshape(query.shape[0], query.shape[1])
    )
    partial_out = jnp.dot(attention, out_weight, preferred_element_type=jnp.float32)
    summed_out = lax.psum(partial_out.astype(jnp.bfloat16), "section")
    return summed_out[None]


CHIPS = 4
VMEM_LIMIT = 56 * 2**20
PIECE = 256


def line(step, sources):
    return [(2 * z + c, 2 * (z + step) + c) for z in sources for c in range(2)]


def nothing(*refs):
    pass


def after(values, done):
    anywhere = pl.BlockSpec(memory_space=pl.ANY)
    count = len(values)
    return pl.pallas_call(
        nothing,
        in_specs=[anywhere] * (count + len(done)),
        out_specs=[anywhere] * count,
        out_shape=[jax.ShapeDtypeStruct(value.shape, value.dtype) for value in values],
        input_output_aliases={k: k for k in range(count)},
        compiler_params=pltpu.CompilerParams(vmem_limit_bytes=2**20),
        name="after",
    )(*values, *done)


def by_chip(z, options):
    picked = options[0]
    for place in range(1, CHIPS):
        if options[place] is not picked:
            picked = jnp.where(z >= place, options[place], picked)
    return picked


def core_swap(value):
    return lax.ppermute(value, "pb", [(p, p ^ 1) for p in range(2 * CHIPS)])


def gather_pieces(own, partner, z, add_pieces, terms, pair_of, questions, other_rows):
    def left(value, sources):
        return lax.ppermute(value, "pb", line(-1, sources))

    def right(value, sources):
        return lax.ppermute(value, "pb", line(1, sources))

    def outward(value):
        return lax.ppermute(value, "pb", line(-1, (1,)) + line(1, (2,)))

    def across(value):
        return lax.ppermute(value, "fsdp", [(0, 1), (1, 0)])

    here, second, third, fourth = (0, 1, 2, 3), (1, 2, 1, 2), (2, 0, 3, 1), (3, 3, 0, 0)

    x_b = across(own)
    l_b1, r_b1 = left(own, (1, 2, 3)), right(own, (0, 1, 2))
    l_a1, r_a1 = left(partner, (1, 2, 3)), right(partner, (0, 1, 2))
    x_a = across(partner)

    both = terms + across(terms)
    pair = pair_of(both)

    l_b2 = left(jnp.where(z == 3, x_b, l_b1), (1, 2, 3))
    r_b2 = right(jnp.where(z == 0, x_b, r_b1), (0, 1, 2))
    l_a2, r_a2 = left(l_a1, (1, 2)), right(r_a1, (1, 2))
    ab1 = jnp.where(z < 2, jnp.concatenate([l_a1, l_b1]), jnp.concatenate([r_a1, r_b1]))
    (ab1,) = after((ab1,), (x_a,))
    x_ab1 = across(ab1)

    l_b3, r_b3 = left(l_b2, (1, 2)), right(r_b2, (1, 2))
    end_a3 = outward(jnp.where(z < 2, l_a2, r_a2))
    a2 = by_chip(z, (l_a2, r_a1, l_a1, r_a2))
    ab2 = jnp.concatenate([a2, jnp.where(z < 2, l_b2, r_b2)])
    x_ab2 = across(ab2)

    def all_z(piece, part=0):
        return ((piece, part),) * 4

    def each_z(*pieces):
        return tuple((piece, 0) for piece in pieces)

    sums, token = add_pieces(
        [
            (all_z(own), here, 0, 0),
            (all_z(partner), here, 0, 1),
            (all_z(x_b), here, 1, 0),
            (all_z(x_a), here, 1, 1),
            (all_z(ab1, 0), second, 0, 1),
            (all_z(ab1, 1), second, 0, 0),
            (all_z(x_ab1, 0), second, 1, 1),
            (all_z(x_ab1, 1), second, 1, 0),
            (all_z(ab2, 0), third, 0, 1),
            (each_z(l_b2, r_b1, l_b1, r_b2), third, 0, 0),
        ],
        None,
    )

    end_a3, l_b3, r_b3 = after((end_a3, l_b3, r_b3), (token,))
    a3 = by_chip(z, (end_a3, l_a2, r_a2, end_a3))
    x_a3 = across(a3)
    end_b4 = outward(jnp.where(z < 2, l_b3, r_b3))
    queries = spread_queries(after((pair,), (token,))[0], questions)

    sums, token = add_pieces(
        [
            (all_z(a3), fourth, 0, 1),
            (each_z(l_b3, l_b2, r_b2, r_b3), fourth, 0, 0),
            (all_z(x_ab2, 0), third, 1, 1),
            (((x_ab2, 1), (r_b2, 0), (l_b2, 0), (x_ab2, 1)), third, 1, 0),
        ],
        sums,
    )
    last = [
        (all_z(x_a3), fourth, 1, 1),
        (each_z(end_b4, l_b3, r_b3, end_b4), fourth, 1, 0),
    ]
    return sums, last, queries


def feature_blocks(pieces, z, c, f):
    found = []
    for _, origins, other_x, other_core in pieces:
        origin = by_chip(z, [jnp.int32(o) for o in origins])
        core = 1 - c if other_core else c
        place = 1 - f if other_x else f
        found.append(4 * origin + 2 * core + place)
    return jnp.stack(found)


def distinct(pieces):
    arrays, wanted = [], []
    for options, _, _, _ in pieces:
        spots = []
        for option, part in options:
            at = next((k for k, seen in enumerate(arrays) if seen is option), None)
            if at is None:
                at = len(arrays)
                arrays.append(option)
            spots.append((at, part))
        wanted.append(spots)
    return arrays, wanted


def load_weights(wanted, z, sources, weights, sems):
    def copy(slot, spot):
        at, part = spot
        return pltpu.make_async_copy(
            sources[at].at[pl.ds(part * PIECE, PIECE)], weights.at[pl.ds(slot * PIECE, PIECE)], sems.at[slot]
        )

    for slot, spots in enumerate(wanted):
        for spot in sorted(set(spots)):
            zs = [k for k, other in enumerate(spots) if other == spot]
            begin = copy(slot, spot).start
            if len(zs) == CHIPS:
                begin()
            else:
                pl.when(functools.reduce(jnp.logical_or, [z == k for k in zs]))(lambda begin=begin: begin())
    for slot, spots in enumerate(wanted):
        copy(slot, spots[0]).wait()


def project_kernel(wanted, amount, carried, info, *refs):
    refs = list(refs)
    count = len(wanted)
    halves, refs = (refs[:count], refs[count : 2 * count]), refs[2 * count :]
    before = refs.pop(0) if carried else None
    sources, (total, token, weights, sems) = refs[:amount], refs[amount:]

    question = pl.program_id(0)

    @pl.when(question == 0)
    def _():
        load_weights(wanted, info[0], sources, weights, sems)
        token[...] = jnp.zeros_like(token)

    for half, blocks in enumerate(halves):
        rows = blocks[0].shape[1]
        here = pl.ds(half * rows, rows)
        features = jnp.concatenate([block[0] for block in blocks], axis=1)
        part = jnp.dot(features, weights[...], preferred_element_type=jnp.float32)
        if carried:
            part = part + before[0, here, :]
        total[0, here, :] = part


def project_pieces(info, pieces, own_rows, other_rows, before=None):
    questions, rows, width = own_rows.shape
    columns = pieces[0][0][0][0].shape[1]
    arrays, wanted = distinct(pieces)
    count = len(pieces)
    carried = before is not None
    blocks = [pl.BlockSpec((1, rows, PIECE), lambda i, info, k=k: (i, 0, info[1 + k])) for k in range(count)]
    sums = pl.BlockSpec((1, 2 * rows, columns), lambda i, info: (i, 0, 0))
    anywhere = pl.BlockSpec(memory_space=pl.ANY)
    return pl.pallas_call(
        functools.partial(project_kernel, wanted, len(arrays), carried),
        grid_spec=pltpu.PrefetchScalarGridSpec(
            num_scalar_prefetch=1,
            grid=(questions,),
            in_specs=blocks + blocks + ([sums] if carried else []) + [anywhere] * len(arrays),
            out_specs=[sums, pl.BlockSpec((8, 128), lambda i, info: (0, 0))],
            scratch_shapes=[
                pltpu.VMEM((count * PIECE, columns), jnp.bfloat16),
                pltpu.SemaphoreType.DMA((count,)),
            ],
        ),
        out_shape=[
            jax.ShapeDtypeStruct((questions, 2 * rows, columns), jnp.float32),
            jax.ShapeDtypeStruct((8, 128), jnp.float32),
        ],
        input_output_aliases={2 * count + 1: 0} if carried else {},
        compiler_params=pltpu.CompilerParams(vmem_limit_bytes=VMEM_LIMIT),
        cost_estimate=pl.CostEstimate(flops=1000, bytes_accessed=1000, transcendentals=0),
        name="project",
    )(info, *([own_rows] * count), *([other_rows] * count), *([before] if carried else []), *arrays)


def attend_kernel(wanted, amount, info, *refs):
    refs = list(refs)
    count = len(wanted)
    halves, refs = (refs[:count], refs[count : 2 * count]), refs[2 * count :]
    before, queries, live, refs = refs[0], refs[1], refs[2], refs[3:]
    sources, refs = refs[:amount], refs[amount:]
    outs, (weights, sems) = refs[:-2], refs[-2:]
    step = pl.program_id(0)

    @pl.when(step == 0)
    def _():
        load_weights(wanted, info[0], sources, weights, sems)

    found = []
    for half, blocks in enumerate(halves):
        rows = blocks[0].shape[1]
        features = jnp.concatenate([block[0] for block in blocks], axis=1)
        part = jnp.dot(features, weights[...], preferred_element_type=jnp.float32)
        found.append((part + before[0, pl.ds(half * rows, rows), :]).astype(jnp.bfloat16))
    keyval = jnp.concatenate(found, axis=0)
    width = keyval.shape[1] // 2
    answers = queries.shape[1]
    group = 4
    span = group * HD
    shown = live[0] > 0
    lane_head = lax.broadcasted_iota(jnp.int32, (answers, span), 1) // HD
    tail_lane = lax.broadcasted_iota(jnp.int32, (answers, 128), 1)
    head_total = width // HD
    extra = jnp.zeros((answers, 128), jnp.float32)
    parts = []
    for g in range(width // span):
        at = slice(g * span, (g + 1) * span)
        query = queries[0, :, at]
        spread = jnp.concatenate(
            [jnp.where(lane_head == h, query, jnp.zeros_like(query)) for h in range(group)], axis=0
        )
        scores = lax.dot_general(
            spread, keyval[:, at], (((1,), (1,)), ((), ())), preferred_element_type=jnp.float32
        )
        scores = jnp.where(shown, scores, NEGATIVE)
        peak = jnp.max(scores, axis=1, keepdims=True)
        raw = jnp.where(shown, jnp.exp(scores - peak), 0.0)
        total = jnp.sum(raw, axis=1, keepdims=True)
        value_at = slice(width + g * span, width + (g + 1) * span)
        numer = jnp.dot(raw.astype(jnp.bfloat16), keyval[:, value_at], preferred_element_type=jnp.float32)
        own = jnp.zeros((answers, span), jnp.float32)
        for h in range(group):
            mine = slice(h * answers, (h + 1) * answers)
            own = jnp.where(lane_head == h, numer[mine], own)
            extra = jnp.where(tail_lane == g * group + h, peak[mine], extra)
            extra = jnp.where(tail_lane == head_total + g * group + h, total[mine], extra)
        parts.append(own)
    result = jnp.concatenate(parts + [extra], axis=1)
    for k, out in enumerate(outs):

        @pl.when(step == k)
        def _(out=out):
            out[...] = result


def attend_last(info, pieces, own_rows, other_rows, before, queries, live, first, amount):
    questions, rows, width = own_rows.shape
    columns = pieces[0][0][0][0].shape[1]
    answers = queries.shape[1]
    arrays, wanted = distinct(pieces)
    count = len(pieces)
    wide = columns // 2 + 128

    def question(i, info):
        return lax.rem(i + first + info[0], questions)

    def turned(i, info):
        wanted = question(i, info)
        pairs = questions // 2
        return 2 * lax.rem(wanted // 2 + info[0] * (pairs - 1), pairs) + lax.rem(wanted, 2)


    blocks = [
        pl.BlockSpec((1, rows, PIECE), lambda i, info, k=k: (question(i, info), 0, info[1 + k]))
        for k in range(count)
    ]
    whole = lambda *shape: pl.BlockSpec((1,) + shape, lambda i, info: (question(i, info), 0, 0))
    anywhere = pl.BlockSpec(memory_space=pl.ANY)
    flops = 4 * amount * rows * count * PIECE * columns + 16 * amount * rows * answers * columns
    return pl.pallas_call(
        functools.partial(attend_kernel, wanted, len(arrays)),
        grid_spec=pltpu.PrefetchScalarGridSpec(
            num_scalar_prefetch=1,
            grid=(amount,),
            in_specs=blocks
            + blocks
            + [
                whole(2 * rows, columns),
                pl.BlockSpec((1, answers, columns // 2), lambda i, info: (turned(i, info), 0, 0)),
                whole(1, 2 * rows),
            ]
            + [anywhere] * len(arrays),
            out_specs=[pl.BlockSpec((answers, wide), lambda i, info: (0, 0))] * amount,
            scratch_shapes=[
                pltpu.VMEM((count * PIECE, columns), jnp.bfloat16),
                pltpu.SemaphoreType.DMA((count,)),
            ],
        ),
        out_shape=[jax.ShapeDtypeStruct((answers, wide), jnp.float32)] * amount,
        compiler_params=pltpu.CompilerParams(vmem_limit_bytes=VMEM_LIMIT),
        cost_estimate=pl.CostEstimate(
            flops=flops,
            bytes_accessed=amount * rows * (8 * columns + 4 * count * PIECE),
            transcendentals=amount * rows * answers * columns // HD,
        ),
        name="attend",
    )(info, *([own_rows] * count), *([other_rows] * count), before, queries, live, *arrays)


def merge_kernel(*refs):
    parts, out = refs[:-1], refs[-1]
    answers, width = out.shape
    heads = width // HD
    lane = lax.broadcasted_iota(jnp.int32, (answers, 128), 1)
    tails = [part[:, pl.ds(width, 128)] for part in parts]
    peak = functools.reduce(jnp.maximum, tails)
    factors = [jnp.exp(jnp.where(lane < heads, tail - peak, 0.0)) for tail in tails]

    def column(value, at):
        return value[:, at : at + 1]

    for tile in range(width // 128):
        low, high = 2 * tile, 2 * tile + 1
        numer = jnp.zeros((answers, 128), jnp.float32)
        total = jnp.zeros((answers, 128), jnp.float32)
        for part, tail, factor in zip(parts, tails, factors):
            scale = jnp.where(lane < HD, column(factor, low), column(factor, high))
            amount = jnp.where(lane < HD, column(tail, heads + low), column(tail, heads + high))
            numer += part[:, pl.ds(tile * 128, 128)] * scale
            total += amount * scale
        out[:, pl.ds(tile * 128, 128)] = (numer / total).astype(out.dtype)


def merge(parts):
    answers, wide = parts[0].shape
    return pl.pallas_call(
        merge_kernel,
        out_shape=jax.ShapeDtypeStruct((answers, wide - 128), jnp.bfloat16),
        cost_estimate=pl.CostEstimate(flops=8 * answers * wide, bytes_accessed=16 * answers * wide, transcendentals=512 * answers),
        compiler_params=pltpu.CompilerParams(vmem_limit_bytes=4 * 2**20),
        name="merge",
    )(*parts)


def query_terms(states, norm_gain, query_weight):
    states_wide = states.astype(jnp.float32)
    square_part = jnp.sum(states_wide * states_wide, axis=1, keepdims=True)
    scaled = (states_wide * norm_gain.astype(jnp.float32)[None, :]).astype(jnp.bfloat16)
    query_part = jnp.dot(scaled, query_weight, preferred_element_type=jnp.float32)
    return jnp.concatenate([query_part, jnp.broadcast_to(square_part, (square_part.shape[0], 128))], axis=1)


def spread_queries(pair, questions):
    pairs = questions // 2
    spread = []
    for turn in range(pairs):
        sends = []
        for place in range(2):
            for to in range(CHIPS):
                chip = pairs * place + (to + turn) % pairs
                for core in range(2):
                    sends.append((2 * (2 * chip + core) + to // pairs, 2 * (2 * to + core) + place))
        spread.append(lax.ppermute(pair, ("pb", "fsdp"), sends))
    return spread


def gathered_shards(
    decoder_states,
    norm_gain,
    query_weight,
    key_weight,
    value_weight,
    out_weight,
    passage_states,
    block_mask,
):
    pb_index = lax.axis_index("pb")
    f = lax.axis_index("fsdp")
    z, c = pb_index // 2, pb_index % 2
    questions, rows, model_width = passage_states.shape
    width = key_weight.shape[1] // 2

    def core_columns(core):
        return jnp.concatenate(
            [lax.dynamic_slice_in_dim(w, core * width, width, 1) for w in (key_weight, value_weight)], axis=1
        )

    own = core_columns(c)
    partner = core_swap(core_columns(1 - c))
    other_rows = core_swap(passage_states)

    def info(pieces):
        return jnp.concatenate([z[None], feature_blocks(pieces, z, c, f)]).astype(jnp.int32)

    def add_pieces(pieces, sums):
        return project_pieces(info(pieces), pieces, passage_states, other_rows, sums)

    terms = query_terms(decoder_states[0], norm_gain, query_weight)

    def pair_of(both):
        query_raw, square_sum = both[:, :-128], both[:, -128:-127]
        query = (query_raw * lax.rsqrt(square_sum / model_width + 1e-06)).astype(jnp.bfloat16)
        mine = lax.dynamic_slice_in_dim(query, c * width, width, 1)
        theirs = core_swap(lax.dynamic_slice_in_dim(query, (1 - c) * width, width, 1))
        return jnp.stack([jnp.where(c == 0, mine, theirs), jnp.where(c == 0, theirs, mine)])

    sums, last, queries = gather_pieces(own, partner, z, add_pieces, terms, pair_of, questions, other_rows)
    queries = jnp.concatenate(queries, axis=0)

    blocks_here = rows // BLOCK
    mine = lax.dynamic_slice_in_dim(block_mask, f * questions, questions, 0)
    live = jnp.concatenate(
        [lax.dynamic_slice_in_dim(mine, p * blocks_here, blocks_here, 1) for p in (pb_index, pb_index ^ 1)],
        axis=1,
    )
    live = jnp.repeat(live, BLOCK, axis=1)[:, None, :]

    def partials(first, amount):
        return attend_last(
            info(last), last, passage_states, other_rows, sums, queries, live, first, amount
        )

    arrived = []
    for step, part in enumerate(partials(1, CHIPS - 1), 1):
        turn = [(2 * k + core, 2 * ((k + step) % CHIPS) + core) for k in range(CHIPS) for core in range(2)]
        arrived.append(lax.ppermute(part, "pb", turn))
    arrived += partials(0, 1)
    attention = merge(arrived)

    received = []
    for flip in range(2):
        sends = [
            (2 * (2 * k + core) + x, 2 * (questions * x + k) + (core ^ flip))
            for k in range(CHIPS)
            for core in range(2)
            for x in range(2)
        ]
        received.append(lax.ppermute(attention, ("pb", "fsdp"), sends))
    first = jnp.where(f == 0, received[0], received[1])
    second = jnp.where(f == 0, received[1], received[0])
    whole = jnp.concatenate([first, second], axis=1)
    partial_out = jnp.dot(whole, out_weight, preferred_element_type=jnp.float32).astype(jnp.bfloat16)
    other_out = lax.ppermute(partial_out, "section", [(0, 1), (1, 0)])
    summed = (partial_out.astype(jnp.float32) + other_out.astype(jnp.float32)).astype(jnp.bfloat16)
    return summed[None]


def solution(mesh):
    placed = (
        P("pb", None, "fsdp"),
        P("fsdp"),
        P("fsdp", "section"),
        P(("pb", "fsdp"), "section"),
        P(("pb", "fsdp"), "section"),
        P("section", "fsdp"),
        P("fsdp", "pb", None),
        P(),
    )
    sizes = dict(mesh.shape)
    fits = sizes == {"section": 2, "pb": 2 * CHIPS, "fsdp": 2}
    return jax.shard_map(
        gathered_shards if fits else plain_shards,
        mesh=mesh,
        in_specs=placed,
        out_specs=P("pb", None, "fsdp"),
        check_vma=False,
    )
```

```python
import functools

import jax
import jax.numpy as jnp
from jax import lax
from jax.experimental import pallas as pl
from jax.experimental.pallas import tpu as pltpu
from jax.sharding import PartitionSpec as P

HD = 64
BLOCK = 128
PASSAGE = 256


NEGATIVE = -1e30


def joined(value, axis, combine):
    everything = jax.tree.map(lambda part: lax.all_gather(part, axis), value)
    leading = jax.tree.map(lambda part: part[0], everything)

    def turn(k, so_far):
        return combine(so_far, jax.tree.map(lambda part: part[k], everything))

    return lax.fori_loop(1, lax.axis_size(axis), turn, leading)


def pack_order(alive_flags):
    amount = alive_flags.shape[0]
    ahead_count = jnp.cumsum(alive_flags) - alive_flags
    behind = jnp.cumsum(1 - alive_flags) - (1 - alive_flags)
    filled = jnp.sum(alive_flags)
    slot_index = jnp.where(alive_flags > 0, ahead_count, filled + behind)
    places = jnp.arange(amount, dtype=jnp.int32)
    order_index = jnp.sum(
        jnp.where(slot_index[None, :] == places[:, None], places[None, :], 0), axis=1
    )
    return (slot_index, order_index, filled)


def project(pieces, alive_flags, stacked):
    amount, piece_rows, model_width = pieces.shape
    slot_index, order_index, filled = pack_order(alive_flags)
    packed = pieces[order_index]
    per_group = min(amount, max(1, 256 // piece_rows))
    columns = stacked.shape[1]

    def compute(row_block):
        return jnp.dot(row_block, stacked, preferred_element_type=jnp.float32).astype(jnp.bfloat16)

    def skipped(row_block):
        return jnp.zeros((row_block.shape[0], columns), jnp.bfloat16)

    def advance(group_index, buffer):
        first_piece = group_index * per_group
        row_block = lax.dynamic_slice_in_dim(packed, first_piece, per_group, 0).reshape(
            per_group * piece_rows, model_width
        )
        result = lax.cond(first_piece < filled, compute, skipped, row_block)
        return lax.dynamic_update_slice_in_dim(
            buffer, result.reshape(per_group, piece_rows, columns), first_piece, 0
        )

    empty_buffer = jnp.zeros((amount, piece_rows, columns), jnp.bfloat16)
    buffer = lax.fori_loop(0, amount // per_group, advance, empty_buffer)
    return (buffer, slot_index, filled)


def attend(query, keyval, live_rows):
    row_total, doubled = keyval.shape
    half_width = doubled // 2
    head_count = half_width // HD
    answer_len = query.shape[0]
    keys_part = keyval[:, :half_width].reshape(row_total, head_count, HD)
    values_part = keyval[:, half_width:].reshape(row_total, head_count, HD)
    queries = query.reshape(answer_len, head_count, HD)
    scores = jnp.einsum("ahd,rhd->ahr", queries, keys_part, preferred_element_type=jnp.float32)
    shown = live_rows[None, None, :]
    scores = jnp.where(shown, scores, NEGATIVE)
    peak = jnp.max(scores, axis=2)
    raw_weights = jnp.where(shown, jnp.exp(scores - peak[:, :, None]), 0.0)
    totals = jnp.sum(raw_weights, axis=2)
    numerator = jnp.einsum(
        "ahr,rhd->ahd",
        raw_weights.astype(jnp.bfloat16),
        values_part,
        preferred_element_type=jnp.float32,
    )
    return (peak, totals, numerator)


def combine_parts(first, second):
    peak_one, totals_one, numer_one = first
    peak_two, totals_two, numer_two = second
    peak = jnp.maximum(peak_one, peak_two)
    factor_one = jnp.exp(peak_one - peak)
    factor_two = jnp.exp(peak_two - peak)
    totals = totals_one * factor_one + totals_two * factor_two
    numerator = numer_one * factor_one[:, :, None] + numer_two * factor_two[:, :, None]
    return (peak, totals, numerator)


def plain_shards(
    decoder_states,
    norm_gain,
    query_weight,
    key_weight,
    value_weight,
    out_weight,
    passage_states,
    block_mask,
):
    pb_count = lax.axis_size("pb")
    fsdp_count = lax.axis_size("fsdp")
    pb_index = lax.axis_index("pb")
    fsdp_index = lax.axis_index("fsdp")
    local_questions, local_rows, model_width = passage_states.shape
    block_total = block_mask.shape[1]
    passages_here = local_rows // PASSAGE
    piece_rows = PASSAGE // fsdp_count
    block_ids = jnp.arange(block_total, dtype=jnp.int32)
    own_mask = lax.dynamic_slice_in_dim(block_mask, pb_index, 1, 0)[0]
    passage_ids = jnp.arange(pb_count * passages_here, dtype=jnp.int32)
    piece_block = (passage_ids * PASSAGE + fsdp_index * piece_rows) // BLOCK
    decoder_live = jnp.sum(
        jnp.where(piece_block[:, None] == block_ids[None, :], own_mask[None, :], 0), axis=1
    )
    stacked_local = jnp.concatenate([key_weight, value_weight], axis=1)
    stacked = lax.all_gather(stacked_local, ("pb", "fsdp"), axis=0, tiled=True)
    own_states = decoder_states[0]
    states_wide = own_states.astype(jnp.float32)
    square_part = jnp.sum(states_wide * states_wide, axis=1)
    scaled = (states_wide * norm_gain.astype(jnp.float32)[None, :]).astype(jnp.bfloat16)
    query_part = jnp.dot(scaled, query_weight, preferred_element_type=jnp.float32)
    square_sum, query_raw = lax.psum((square_part, query_part), "fsdp")
    query = (query_raw * lax.rsqrt(square_sum / model_width + 1e-06)[:, None]).astype(jnp.bfloat16)
    shaped = passage_states.reshape(
        local_questions, passages_here, fsdp_count, piece_rows, model_width
    )
    by_piece = lax.all_to_all(shaped, "fsdp", split_axis=2, concat_axis=0, tiled=True)
    by_question = lax.all_to_all(by_piece, "pb", split_axis=0, concat_axis=1, tiled=True)
    pieces = by_question.reshape(pb_count * passages_here, piece_rows, model_width)
    projected, slot_index, filled = project(pieces, decoder_live, stacked)
    keyval = projected.reshape(pb_count * passages_here * piece_rows, projected.shape[2])
    live_rows = jnp.repeat(passage_ids < filled, piece_rows)
    peak, totals, numerator = attend(query, keyval, live_rows)
    peak, totals, numerator = joined((peak, totals, numerator), "fsdp", combine_parts)
    attention = (
        (numerator / totals[:, :, None])
        .astype(jnp.bfloat16)
        .reshape(query.shape[0], query.shape[1])
    )
    partial_out = jnp.dot(attention, out_weight, preferred_element_type=jnp.float32)
    summed_out = lax.psum(partial_out.astype(jnp.bfloat16), "section")
    return summed_out[None]


CHIPS = 4
VMEM_LIMIT = 44 * 2**20
PIECE = 256


def line(step, sources):
    return [(2 * z + c, 2 * (z + step) + c) for z in sources for c in range(2)]


def nothing(*refs):
    pass


def after(values, done):
    anywhere = pl.BlockSpec(memory_space=pl.ANY)
    count = len(values)
    return pl.pallas_call(
        nothing,
        in_specs=[anywhere] * (count + len(done)),
        out_specs=[anywhere] * count,
        out_shape=[jax.ShapeDtypeStruct(value.shape, value.dtype) for value in values],
        input_output_aliases={k: k for k in range(count)},
        compiler_params=pltpu.CompilerParams(vmem_limit_bytes=2**20),
        name="after",
    )(*values, *done)


def by_chip(z, options):
    picked = options[0]
    for place in range(1, CHIPS):
        if options[place] is not picked:
            picked = jnp.where(z >= place, options[place], picked)
    return picked


def core_swap(value):
    return lax.ppermute(value, "pb", [(p, p ^ 1) for p in range(2 * CHIPS)])


def gather_pieces(own, partner, z, add_pieces, terms, pair_of, questions, ready):
    def left(value, sources):
        return lax.ppermute(value, "pb", line(-1, sources))

    def right(value, sources):
        return lax.ppermute(value, "pb", line(1, sources))

    def outward(value):
        return lax.ppermute(value, "pb", line(-1, (1,)) + line(1, (2,)))

    def across(value):
        return lax.ppermute(value, "fsdp", [(0, 1), (1, 0)])

    here, second, third, fourth = (0, 1, 2, 3), (1, 2, 1, 2), (2, 0, 3, 1), (3, 3, 0, 0)

    x_b = across(own)
    l_b1, r_b1 = left(own, (1, 2, 3)), right(own, (0, 1, 2))
    l_a1, r_a1 = left(partner, (1, 2, 3)), right(partner, (0, 1, 2))
    x_a = across(partner)

    both = terms + across(terms)
    pair = pair_of(both)

    l_b2 = left(jnp.where(z == 3, x_b, l_b1), (1, 2, 3))
    r_b2 = right(jnp.where(z == 0, x_b, r_b1), (0, 1, 2))
    l_a2, r_a2 = left(l_a1, (1, 2)), right(r_a1, (1, 2))
    ab1 = jnp.where(z < 2, jnp.concatenate([l_a1, l_b1]), jnp.concatenate([r_a1, r_b1]))
    (ab1,) = after((ab1,), (x_a,))
    x_ab1 = across(ab1)

    l_b3, r_b3 = left(l_b2, (1, 2)), right(r_b2, (1, 2))
    end_a3 = outward(jnp.where(z < 2, l_a2, r_a2))
    a2 = by_chip(z, (l_a2, r_a1, l_a1, r_a2))
    ab2 = jnp.concatenate([a2, jnp.where(z < 2, l_b2, r_b2)])
    x_ab2 = across(ab2)

    def all_z(piece, part=0):
        return ((piece, part),) * 4

    def each_z(*pieces):
        return tuple((piece, 0) for piece in pieces)

    sums, token = add_pieces(
        [
            (all_z(own), here, 0, 0),
            (all_z(partner), here, 0, 1),
            (all_z(x_b), here, 1, 0),
            (all_z(x_a), here, 1, 1),
            (all_z(ab1, 0), second, 0, 1),
            (all_z(ab1, 1), second, 0, 0),
            (all_z(x_ab1, 0), second, 1, 1),
            (all_z(x_ab1, 1), second, 1, 0),
            (all_z(ab2, 0), third, 0, 1),
            (each_z(l_b2, r_b1, l_b1, r_b2), third, 0, 0),
        ],
        None,
    )

    end_a3, l_b3, r_b3 = after((end_a3, l_b3, r_b3), (token, *ready))
    a3 = by_chip(z, (end_a3, l_a2, r_a2, end_a3))
    x_a3 = across(a3)
    end_b4 = outward(jnp.where(z < 2, l_b3, r_b3))
    queries = spread_queries(after((pair,), (token,))[0], questions)

    sums, token = add_pieces(
        [
            (all_z(a3), fourth, 0, 1),
            (each_z(l_b3, l_b2, r_b2, r_b3), fourth, 0, 0),
            (all_z(x_ab2, 0), third, 1, 1),
            (((x_ab2, 1), (r_b2, 0), (l_b2, 0), (x_ab2, 1)), third, 1, 0),
        ],
        sums,
    )
    last = [
        (all_z(x_a3), fourth, 1, 1),
        (each_z(end_b4, l_b3, r_b3, end_b4), fourth, 1, 0),
    ]
    return sums, last, queries


def feature_blocks(pieces, z, c, f):
    found = []
    for _, origins, other_x, other_core in pieces:
        origin = by_chip(z, [jnp.int32(o) for o in origins])
        core = 1 - c if other_core else c
        place = 1 - f if other_x else f
        found.append(4 * origin + 2 * core + place)
    return jnp.stack(found)


def distinct(pieces):
    arrays, wanted = [], []
    for options, _, _, _ in pieces:
        spots = []
        for option, part in options:
            at = next((k for k, seen in enumerate(arrays) if seen is option), None)
            if at is None:
                at = len(arrays)
                arrays.append(option)
            spots.append((at, part))
        wanted.append(spots)
    return arrays, wanted


def load_weights(wanted, z, sources, weights, sems):
    def copy(slot, spot):
        at, part = spot
        return pltpu.make_async_copy(
            sources[at].at[pl.ds(part * PIECE, PIECE)], weights.at[pl.ds(slot * PIECE, PIECE)], sems.at[slot]
        )

    for slot, spots in enumerate(wanted):
        for spot in sorted(set(spots)):
            zs = [k for k, other in enumerate(spots) if other == spot]
            begin = copy(slot, spot).start
            if len(zs) == CHIPS:
                begin()
            else:
                pl.when(functools.reduce(jnp.logical_or, [z == k for k in zs]))(lambda begin=begin: begin())
    for slot, spots in enumerate(wanted):
        copy(slot, spots[0]).wait()


def project_kernel(wanted, amount, carried, info, *refs):
    refs = list(refs)
    count = len(wanted)
    halves, refs = (refs[:count], refs[count : 2 * count]), refs[2 * count :]
    before = refs.pop(0) if carried else None
    sources, (total, token, weights, sems) = refs[:amount], refs[amount:]

    question = pl.program_id(0)

    @pl.when(question == 0)
    def _():
        load_weights(wanted, info[0], sources, weights, sems)
        token[...] = jnp.zeros_like(token)

    for half, blocks in enumerate(halves):
        rows = blocks[0].shape[1]
        here = pl.ds(half * rows, rows)
        features = jnp.concatenate([block[0] for block in blocks], axis=1)
        part = jnp.dot(features, weights[...], preferred_element_type=jnp.float32)
        if carried:
            part = part + before[0, here, :]
        total[0, here, :] = part


def project_pieces(info, pieces, own_rows, other_rows, before=None):
    questions, rows, width = own_rows.shape
    columns = pieces[0][0][0][0].shape[1]
    arrays, wanted = distinct(pieces)
    count = len(pieces)
    carried = before is not None
    blocks = [pl.BlockSpec((1, rows, PIECE), lambda i, info, k=k: (i, 0, info[1 + k])) for k in range(count)]
    sums = pl.BlockSpec((1, 2 * rows, columns), lambda i, info: (i, 0, 0))
    anywhere = pl.BlockSpec(memory_space=pl.ANY)
    return pl.pallas_call(
        functools.partial(project_kernel, wanted, len(arrays), carried),
        grid_spec=pltpu.PrefetchScalarGridSpec(
            num_scalar_prefetch=1,
            grid=(questions,),
            in_specs=blocks + blocks + ([sums] if carried else []) + [anywhere] * len(arrays),
            out_specs=[sums, pl.BlockSpec((8, 128), lambda i, info: (0, 0))],
            scratch_shapes=[
                pltpu.VMEM((count * PIECE, columns), jnp.bfloat16),
                pltpu.SemaphoreType.DMA((count,)),
            ],
        ),
        out_shape=[
            jax.ShapeDtypeStruct((questions, 2 * rows, columns), jnp.float32),
            jax.ShapeDtypeStruct((8, 128), jnp.float32),
        ],
        input_output_aliases={2 * count + 1: 0} if carried else {},
        compiler_params=pltpu.CompilerParams(vmem_limit_bytes=VMEM_LIMIT),
        cost_estimate=pl.CostEstimate(flops=1000, bytes_accessed=1000, transcendentals=0),
        name="project",
    )(info, *([own_rows] * count), *([other_rows] * count), *([before] if carried else []), *arrays)


def attend_kernel(wanted, amount, info, *refs):
    refs = list(refs)
    count = len(wanted)
    halves, refs = (refs[:count], refs[count : 2 * count]), refs[2 * count :]
    before, queries, live, refs = refs[0], refs[1], refs[2], refs[3:]
    sources, refs = refs[:amount], refs[amount:]
    outs, (weights, sems) = refs[:-2], refs[-2:]
    step = pl.program_id(0)

    @pl.when(step == 0)
    def _():
        load_weights(wanted, info[0], sources, weights, sems)

    found = []
    for half, blocks in enumerate(halves):
        rows = blocks[0].shape[1]
        features = jnp.concatenate([block[0] for block in blocks], axis=1)
        part = jnp.dot(features, weights[...], preferred_element_type=jnp.float32)
        found.append((part + before[0, pl.ds(half * rows, rows), :]).astype(jnp.bfloat16))
    keyval = jnp.concatenate(found, axis=0)
    width = keyval.shape[1] // 2
    answers = queries.shape[1]
    group = 4
    span = group * HD
    shown = live[0] > 0
    lane_head = lax.broadcasted_iota(jnp.int32, (answers, span), 1) // HD
    tail_lane = lax.broadcasted_iota(jnp.int32, (answers, 128), 1)
    head_total = width // HD
    extra = jnp.zeros((answers, 128), jnp.float32)
    parts = []
    for g in range(width // span):
        at = slice(g * span, (g + 1) * span)
        query = queries[0, :, at]
        spread = jnp.concatenate(
            [jnp.where(lane_head == h, query, jnp.zeros_like(query)) for h in range(group)], axis=0
        )
        scores = lax.dot_general(
            spread, keyval[:, at], (((1,), (1,)), ((), ())), preferred_element_type=jnp.float32
        )
        scores = jnp.where(shown, scores, NEGATIVE)
        peak = jnp.max(scores, axis=1, keepdims=True)
        raw = jnp.where(shown, jnp.exp(scores - peak), 0.0)
        total = jnp.sum(raw, axis=1, keepdims=True)
        value_at = slice(width + g * span, width + (g + 1) * span)
        numer = jnp.dot(raw.astype(jnp.bfloat16), keyval[:, value_at], preferred_element_type=jnp.float32)
        own = jnp.zeros((answers, span), jnp.float32)
        for h in range(group):
            mine = slice(h * answers, (h + 1) * answers)
            own = jnp.where(lane_head == h, numer[mine], own)
            extra = jnp.where(tail_lane == g * group + h, peak[mine], extra)
            extra = jnp.where(tail_lane == head_total + g * group + h, total[mine], extra)
        parts.append(own)
    result = jnp.concatenate(parts + [extra], axis=1)
    for k, out in enumerate(outs):

        @pl.when(step == k)
        def _(out=out):
            out[...] = result


def attend_last(info, pieces, own_rows, other_rows, before, queries, live, first, amount):
    questions, rows, width = own_rows.shape
    columns = pieces[0][0][0][0].shape[1]
    answers = queries.shape[1]
    arrays, wanted = distinct(pieces)
    count = len(pieces)
    wide = columns // 2 + 128

    def question(i, info):
        return lax.rem(i + first + info[0], questions)

    def turned(i, info):
        wanted = question(i, info)
        pairs = questions // 2
        return 2 * lax.rem(wanted // 2 + info[0] * (pairs - 1), pairs) + lax.rem(wanted, 2)


    blocks = [
        pl.BlockSpec((1, rows, PIECE), lambda i, info, k=k: (question(i, info), 0, info[1 + k]))
        for k in range(count)
    ]
    whole = lambda *shape: pl.BlockSpec((1,) + shape, lambda i, info: (question(i, info), 0, 0))
    anywhere = pl.BlockSpec(memory_space=pl.ANY)
    flops = 4 * amount * rows * count * PIECE * columns + 16 * amount * rows * answers * columns
    return pl.pallas_call(
        functools.partial(attend_kernel, wanted, len(arrays)),
        grid_spec=pltpu.PrefetchScalarGridSpec(
            num_scalar_prefetch=1,
            grid=(amount,),
            in_specs=blocks
            + blocks
            + [
                whole(2 * rows, columns),
                pl.BlockSpec((1, answers, columns // 2), lambda i, info: (turned(i, info), 0, 0)),
                whole(1, 2 * rows),
            ]
            + [anywhere] * len(arrays),
            out_specs=[pl.BlockSpec((answers, wide), lambda i, info: (0, 0))] * amount,
            scratch_shapes=[
                pltpu.VMEM((count * PIECE, columns), jnp.bfloat16),
                pltpu.SemaphoreType.DMA((count,)),
            ],
        ),
        out_shape=[jax.ShapeDtypeStruct((answers, wide), jnp.float32)] * amount,
        compiler_params=pltpu.CompilerParams(vmem_limit_bytes=VMEM_LIMIT),
        cost_estimate=pl.CostEstimate(
            flops=flops,
            bytes_accessed=amount * rows * (8 * columns + 4 * count * PIECE),
            transcendentals=amount * rows * answers * columns // HD,
        ),
        name="attend",
    )(info, *([own_rows] * count), *([other_rows] * count), before, queries, live, *arrays)


def merge_kernel(*refs):
    parts, out = refs[:-1], refs[-1]
    answers, width = out.shape
    heads = width // HD
    lane = lax.broadcasted_iota(jnp.int32, (answers, 128), 1)
    tails = [part[:, pl.ds(width, 128)] for part in parts]
    peak = functools.reduce(jnp.maximum, tails)
    factors = [jnp.exp(jnp.where(lane < heads, tail - peak, 0.0)) for tail in tails]

    def column(value, at):
        return value[:, at : at + 1]

    for tile in range(width // 128):
        low, high = 2 * tile, 2 * tile + 1
        numer = jnp.zeros((answers, 128), jnp.float32)
        total = jnp.zeros((answers, 128), jnp.float32)
        for part, tail, factor in zip(parts, tails, factors):
            scale = jnp.where(lane < HD, column(factor, low), column(factor, high))
            amount = jnp.where(lane < HD, column(tail, heads + low), column(tail, heads + high))
            numer += part[:, pl.ds(tile * 128, 128)] * scale
            total += amount * scale
        out[:, pl.ds(tile * 128, 128)] = (numer / total).astype(out.dtype)


def merge(parts):
    answers, wide = parts[0].shape
    return pl.pallas_call(
        merge_kernel,
        out_shape=jax.ShapeDtypeStruct((answers, wide - 128), jnp.bfloat16),
        cost_estimate=pl.CostEstimate(flops=8 * answers * wide, bytes_accessed=16 * answers * wide, transcendentals=512 * answers),
        compiler_params=pltpu.CompilerParams(vmem_limit_bytes=4 * 2**20),
        name="merge",
    )(*parts)


def hold_kernel(weights, ready, out, sem):
    copy = pltpu.make_async_copy(weights, out, sem)
    copy.start()
    copy.wait()


def hold(weights, ready):
    anywhere = pl.BlockSpec(memory_space=pl.ANY)
    return pl.pallas_call(
        hold_kernel,
        in_specs=[anywhere, anywhere],
        out_specs=pl.BlockSpec(memory_space=pltpu.VMEM),
        out_shape=pltpu.VMEM(weights.shape, weights.dtype),
        scratch_shapes=[pltpu.SemaphoreType.DMA],
        compiler_params=pltpu.CompilerParams(vmem_limit_bytes=2**20),
        cost_estimate=pl.CostEstimate(flops=0, bytes_accessed=2 * weights.size, transcendentals=0),
        name="hold",
    )(weights, ready)


def output_kernel(place, weights, first, second, out):
    width = first.shape[1]
    total = jnp.zeros(out.shape, jnp.float32)
    for part, core in ((first, place[0]), (second, 1 - place[0])):
        rows = weights[pl.ds(pl.multiple_of(core * width, width), width), :]
        total += jnp.dot(part[...], rows, preferred_element_type=jnp.float32)
    out[...] = total.astype(out.dtype)


def output_terms(place, weights, first, second):
    inside = pl.BlockSpec(memory_space=pltpu.VMEM)
    answers, columns = first.shape[0], weights.shape[1]
    return pl.pallas_call(
        output_kernel,
        in_specs=[pl.BlockSpec(memory_space=pltpu.SMEM), inside, inside, inside],
        out_specs=inside,
        out_shape=jax.ShapeDtypeStruct((answers, columns), jnp.bfloat16),
        compiler_params=pltpu.CompilerParams(vmem_limit_bytes=16 * 2**20),
        cost_estimate=pl.CostEstimate(
            flops=2 * answers * weights.size, bytes_accessed=4 * answers * columns, transcendentals=0
        ),
        name="output",
    )(place, weights, first, second)


def query_terms(states, norm_gain, query_weight):
    states_wide = states.astype(jnp.float32)
    square_part = jnp.sum(states_wide * states_wide, axis=1, keepdims=True)
    scaled = (states_wide * norm_gain.astype(jnp.float32)[None, :]).astype(jnp.bfloat16)
    query_part = jnp.dot(scaled, query_weight, preferred_element_type=jnp.float32)
    return jnp.concatenate([query_part, jnp.broadcast_to(square_part, (square_part.shape[0], 128))], axis=1)


def spread_queries(pair, questions):
    pairs = questions // 2
    spread = []
    for turn in range(pairs):
        sends = []
        for place in range(2):
            for to in range(CHIPS):
                chip = pairs * place + (to + turn) % pairs
                for core in range(2):
                    sends.append((2 * (2 * chip + core) + to // pairs, 2 * (2 * to + core) + place))
        spread.append(lax.ppermute(pair, ("pb", "fsdp"), sends))
    return spread


def gathered_shards(
    decoder_states,
    norm_gain,
    query_weight,
    key_weight,
    value_weight,
    out_weight,
    passage_states,
    block_mask,
):
    pb_index = lax.axis_index("pb")
    f = lax.axis_index("fsdp")
    z, c = pb_index // 2, pb_index % 2
    questions, rows, model_width = passage_states.shape
    width = key_weight.shape[1] // 2

    def core_columns(core):
        return jnp.concatenate(
            [lax.dynamic_slice_in_dim(w, core * width, width, 1) for w in (key_weight, value_weight)], axis=1
        )

    own = core_columns(c)
    partner = core_swap(core_columns(1 - c))
    other_rows = core_swap(passage_states)

    def info(pieces):
        return jnp.concatenate([z[None], feature_blocks(pieces, z, c, f)]).astype(jnp.int32)

    def add_pieces(pieces, sums):
        return project_pieces(info(pieces), pieces, passage_states, other_rows, sums)

    terms = query_terms(decoder_states[0], norm_gain, query_weight)

    def pair_of(both):
        query_raw, square_sum = both[:, :-128], both[:, -128:-127]
        query = (query_raw * lax.rsqrt(square_sum / model_width + 1e-06)).astype(jnp.bfloat16)
        mine = lax.dynamic_slice_in_dim(query, c * width, width, 1)
        theirs = core_swap(lax.dynamic_slice_in_dim(query, (1 - c) * width, width, 1))
        return jnp.stack([jnp.where(c == 0, mine, theirs), jnp.where(c == 0, theirs, mine)])

    blocks_here = rows // BLOCK
    mine = lax.dynamic_slice_in_dim(block_mask, f * questions, questions, 0)
    live = jnp.concatenate(
        [lax.dynamic_slice_in_dim(mine, p * blocks_here, blocks_here, 1) for p in (pb_index, pb_index ^ 1)],
        axis=1,
    )
    live = jnp.repeat(live, BLOCK, axis=1)[:, None, :]

    sums, last, queries = gather_pieces(own, partner, z, add_pieces, terms, pair_of, questions, (live,))
    queries = jnp.concatenate(queries, axis=0)


    def partials(first, amount):
        return attend_last(
            info(last), last, passage_states, other_rows, sums, queries, live, first, amount
        )

    arrived = []
    for step, part in enumerate(partials(1, CHIPS - 1), 1):
        turn = [(2 * k + core, 2 * ((k + step) % CHIPS) + core) for k in range(CHIPS) for core in range(2)]
        arrived.append(lax.ppermute(part, "pb", turn))
    arrived += partials(0, 1)
    attention = merge(arrived)

    received = []
    for flip in range(2):
        sends = [
            (2 * (2 * k + core) + x, 2 * (questions * x + k) + (core ^ flip))
            for k in range(CHIPS)
            for core in range(2)
            for x in range(2)
        ]
        received.append(lax.ppermute(attention, ("pb", "fsdp"), sends))
    partial_out = output_terms(f[None].astype(jnp.int32), hold(out_weight, attention), *received)
    other_out = lax.ppermute(partial_out, "section", [(0, 1), (1, 0)])
    summed = (partial_out.astype(jnp.float32) + other_out.astype(jnp.float32)).astype(jnp.bfloat16)
    return summed[None]


def solution(mesh):
    placed = (
        P("pb", None, "fsdp"),
        P("fsdp"),
        P("fsdp", "section"),
        P(("pb", "fsdp"), "section"),
        P(("pb", "fsdp"), "section"),
        P("section", "fsdp"),
        P("fsdp", "pb", None),
        P(),
    )
    sizes = dict(mesh.shape)
    fits = sizes == {"section": 2, "pb": 2 * CHIPS, "fsdp": 2}
    return jax.shard_map(
        gathered_shards if fits else plain_shards,
        mesh=mesh,
        in_specs=placed,
        out_specs=P("pb", None, "fsdp"),
        check_vma=False,
    )
```

```python
import functools

import jax
import jax.numpy as jnp
from jax import lax
from jax.experimental import pallas as pl
from jax.experimental.pallas import tpu as pltpu
from jax.sharding import PartitionSpec as P

HD = 64
BLOCK = 128
PASSAGE = 256


NEGATIVE = -1e30


def joined(value, axis, combine):
    everything = jax.tree.map(lambda part: lax.all_gather(part, axis), value)
    leading = jax.tree.map(lambda part: part[0], everything)

    def turn(k, so_far):
        return combine(so_far, jax.tree.map(lambda part: part[k], everything))

    return lax.fori_loop(1, lax.axis_size(axis), turn, leading)


def pack_order(alive_flags):
    amount = alive_flags.shape[0]
    ahead_count = jnp.cumsum(alive_flags) - alive_flags
    behind = jnp.cumsum(1 - alive_flags) - (1 - alive_flags)
    filled = jnp.sum(alive_flags)
    slot_index = jnp.where(alive_flags > 0, ahead_count, filled + behind)
    places = jnp.arange(amount, dtype=jnp.int32)
    order_index = jnp.sum(
        jnp.where(slot_index[None, :] == places[:, None], places[None, :], 0), axis=1
    )
    return (slot_index, order_index, filled)


def project(pieces, alive_flags, stacked):
    amount, piece_rows, model_width = pieces.shape
    slot_index, order_index, filled = pack_order(alive_flags)
    packed = pieces[order_index]
    per_group = min(amount, max(1, 256 // piece_rows))
    columns = stacked.shape[1]

    def compute(row_block):
        return jnp.dot(row_block, stacked, preferred_element_type=jnp.float32).astype(jnp.bfloat16)

    def skipped(row_block):
        return jnp.zeros((row_block.shape[0], columns), jnp.bfloat16)

    def advance(group_index, buffer):
        first_piece = group_index * per_group
        row_block = lax.dynamic_slice_in_dim(packed, first_piece, per_group, 0).reshape(
            per_group * piece_rows, model_width
        )
        result = lax.cond(first_piece < filled, compute, skipped, row_block)
        return lax.dynamic_update_slice_in_dim(
            buffer, result.reshape(per_group, piece_rows, columns), first_piece, 0
        )

    empty_buffer = jnp.zeros((amount, piece_rows, columns), jnp.bfloat16)
    buffer = lax.fori_loop(0, amount // per_group, advance, empty_buffer)
    return (buffer, slot_index, filled)


def attend(query, keyval, live_rows):
    row_total, doubled = keyval.shape
    half_width = doubled // 2
    head_count = half_width // HD
    answer_len = query.shape[0]
    keys_part = keyval[:, :half_width].reshape(row_total, head_count, HD)
    values_part = keyval[:, half_width:].reshape(row_total, head_count, HD)
    queries = query.reshape(answer_len, head_count, HD)
    scores = jnp.einsum("ahd,rhd->ahr", queries, keys_part, preferred_element_type=jnp.float32)
    shown = live_rows[None, None, :]
    scores = jnp.where(shown, scores, NEGATIVE)
    peak = jnp.max(scores, axis=2)
    raw_weights = jnp.where(shown, jnp.exp(scores - peak[:, :, None]), 0.0)
    totals = jnp.sum(raw_weights, axis=2)
    numerator = jnp.einsum(
        "ahr,rhd->ahd",
        raw_weights.astype(jnp.bfloat16),
        values_part,
        preferred_element_type=jnp.float32,
    )
    return (peak, totals, numerator)


def combine_parts(first, second):
    peak_one, totals_one, numer_one = first
    peak_two, totals_two, numer_two = second
    peak = jnp.maximum(peak_one, peak_two)
    factor_one = jnp.exp(peak_one - peak)
    factor_two = jnp.exp(peak_two - peak)
    totals = totals_one * factor_one + totals_two * factor_two
    numerator = numer_one * factor_one[:, :, None] + numer_two * factor_two[:, :, None]
    return (peak, totals, numerator)


def plain_shards(
    decoder_states,
    norm_gain,
    query_weight,
    key_weight,
    value_weight,
    out_weight,
    passage_states,
    block_mask,
):
    pb_count = lax.axis_size("pb")
    fsdp_count = lax.axis_size("fsdp")
    pb_index = lax.axis_index("pb")
    fsdp_index = lax.axis_index("fsdp")
    local_questions, local_rows, model_width = passage_states.shape
    block_total = block_mask.shape[1]
    passages_here = local_rows // PASSAGE
    piece_rows = PASSAGE // fsdp_count
    block_ids = jnp.arange(block_total, dtype=jnp.int32)
    own_mask = lax.dynamic_slice_in_dim(block_mask, pb_index, 1, 0)[0]
    passage_ids = jnp.arange(pb_count * passages_here, dtype=jnp.int32)
    piece_block = (passage_ids * PASSAGE + fsdp_index * piece_rows) // BLOCK
    decoder_live = jnp.sum(
        jnp.where(piece_block[:, None] == block_ids[None, :], own_mask[None, :], 0), axis=1
    )
    stacked_local = jnp.concatenate([key_weight, value_weight], axis=1)
    stacked = lax.all_gather(stacked_local, ("pb", "fsdp"), axis=0, tiled=True)
    own_states = decoder_states[0]
    states_wide = own_states.astype(jnp.float32)
    square_part = jnp.sum(states_wide * states_wide, axis=1)
    scaled = (states_wide * norm_gain.astype(jnp.float32)[None, :]).astype(jnp.bfloat16)
    query_part = jnp.dot(scaled, query_weight, preferred_element_type=jnp.float32)
    square_sum, query_raw = lax.psum((square_part, query_part), "fsdp")
    query = (query_raw * lax.rsqrt(square_sum / model_width + 1e-06)[:, None]).astype(jnp.bfloat16)
    shaped = passage_states.reshape(
        local_questions, passages_here, fsdp_count, piece_rows, model_width
    )
    by_piece = lax.all_to_all(shaped, "fsdp", split_axis=2, concat_axis=0, tiled=True)
    by_question = lax.all_to_all(by_piece, "pb", split_axis=0, concat_axis=1, tiled=True)
    pieces = by_question.reshape(pb_count * passages_here, piece_rows, model_width)
    projected, slot_index, filled = project(pieces, decoder_live, stacked)
    keyval = projected.reshape(pb_count * passages_here * piece_rows, projected.shape[2])
    live_rows = jnp.repeat(passage_ids < filled, piece_rows)
    peak, totals, numerator = attend(query, keyval, live_rows)
    peak, totals, numerator = joined((peak, totals, numerator), "fsdp", combine_parts)
    attention = (
        (numerator / totals[:, :, None])
        .astype(jnp.bfloat16)
        .reshape(query.shape[0], query.shape[1])
    )
    partial_out = jnp.dot(attention, out_weight, preferred_element_type=jnp.float32)
    summed_out = lax.psum(partial_out.astype(jnp.bfloat16), "section")
    return summed_out[None]


CHIPS = 4
VMEM_LIMIT = 44 * 2**20
PIECE = 256


def line(step, sources):
    return [(2 * z + c, 2 * (z + step) + c) for z in sources for c in range(2)]


def nothing(*refs):
    pass


def after(values, done):
    anywhere = pl.BlockSpec(memory_space=pl.ANY)
    count = len(values)
    return pl.pallas_call(
        nothing,
        in_specs=[anywhere] * (count + len(done)),
        out_specs=[anywhere] * count,
        out_shape=[jax.ShapeDtypeStruct(value.shape, value.dtype) for value in values],
        input_output_aliases={k: k for k in range(count)},
        compiler_params=pltpu.CompilerParams(vmem_limit_bytes=2**20),
        name="after",
    )(*values, *done)


def by_chip(z, options):
    picked = options[0]
    for place in range(1, CHIPS):
        if options[place] is not picked:
            picked = jnp.where(z >= place, options[place], picked)
    return picked


def core_swap(value):
    return lax.ppermute(value, "pb", [(p, p ^ 1) for p in range(2 * CHIPS)])


def gather_pieces(own, partner, z, add_pieces, terms, pair_of, questions, ready):
    def left(value, sources):
        return lax.ppermute(value, "pb", line(-1, sources))

    def right(value, sources):
        return lax.ppermute(value, "pb", line(1, sources))

    def outward(value):
        return lax.ppermute(value, "pb", line(-1, (1,)) + line(1, (2,)))

    def across(value):
        return lax.ppermute(value, "fsdp", [(0, 1), (1, 0)])

    here, second, third, fourth = (0, 1, 2, 3), (1, 2, 1, 2), (2, 0, 3, 1), (3, 3, 0, 0)

    x_b = across(own)
    l_b1, r_b1 = left(own, (1, 2, 3)), right(own, (0, 1, 2))
    l_a1, r_a1 = left(partner, (1, 2, 3)), right(partner, (0, 1, 2))
    x_a = across(partner)

    both = terms + across(terms)
    pair = pair_of(both)

    l_b2 = left(jnp.where(z == 3, x_b, l_b1), (1, 2, 3))
    r_b2 = right(jnp.where(z == 0, x_b, r_b1), (0, 1, 2))
    l_a2, r_a2 = left(l_a1, (1, 2)), right(r_a1, (1, 2))
    ab1 = jnp.where(z < 2, jnp.concatenate([l_a1, l_b1]), jnp.concatenate([r_a1, r_b1]))
    (ab1,) = after((ab1,), (x_a,))
    x_ab1 = across(ab1)

    l_b3, r_b3 = left(l_b2, (1, 2)), right(r_b2, (1, 2))
    end_a3 = outward(jnp.where(z < 2, l_a2, r_a2))
    a2 = by_chip(z, (l_a2, r_a1, l_a1, r_a2))
    ab2 = jnp.concatenate([a2, jnp.where(z < 2, l_b2, r_b2)])
    x_ab2 = across(ab2)

    def all_z(piece, part=0):
        return ((piece, part),) * 4

    def each_z(*pieces):
        return tuple((piece, 0) for piece in pieces)

    sums, token = add_pieces(
        [
            (all_z(own), here, 0, 0),
            (all_z(partner), here, 0, 1),
            (all_z(x_b), here, 1, 0),
            (all_z(x_a), here, 1, 1),
            (all_z(ab1, 0), second, 0, 1),
            (all_z(ab1, 1), second, 0, 0),
            (all_z(x_ab1, 0), second, 1, 1),
            (all_z(x_ab1, 1), second, 1, 0),
            (all_z(ab2, 0), third, 0, 1),
            (each_z(l_b2, r_b1, l_b1, r_b2), third, 0, 0),
        ],
        None,
    )

    end_a3, l_b3, r_b3 = after((end_a3, l_b3, r_b3), (token, *ready))
    a3 = by_chip(z, (end_a3, l_a2, r_a2, end_a3))
    x_a3 = across(a3)
    end_b4 = outward(jnp.where(z < 2, l_b3, r_b3))
    queries = spread_queries(after((pair,), (token,))[0], questions)

    sums, token = add_pieces(
        [
            (all_z(a3), fourth, 0, 1),
            (each_z(l_b3, l_b2, r_b2, r_b3), fourth, 0, 0),
            (all_z(x_ab2, 0), third, 1, 1),
            (((x_ab2, 1), (r_b2, 0), (l_b2, 0), (x_ab2, 1)), third, 1, 0),
        ],
        sums,
    )
    last = [
        (all_z(x_a3), fourth, 1, 1),
        (each_z(end_b4, l_b3, r_b3, end_b4), fourth, 1, 0),
    ]
    return sums, last, queries


def feature_blocks(pieces, z, c, f):
    found = []
    for _, origins, other_x, other_core in pieces:
        origin = by_chip(z, [jnp.int32(o) for o in origins])
        core = 1 - c if other_core else c
        place = 1 - f if other_x else f
        found.append(4 * origin + 2 * core + place)
    return jnp.stack(found)


def distinct(pieces):
    arrays, wanted = [], []
    for options, _, _, _ in pieces:
        spots = []
        for option, part in options:
            at = next((k for k, seen in enumerate(arrays) if seen is option), None)
            if at is None:
                at = len(arrays)
                arrays.append(option)
            spots.append((at, part))
        wanted.append(spots)
    return arrays, wanted


def load_weights(wanted, z, sources, weights, sems):
    def copy(slot, spot):
        at, part = spot
        return pltpu.make_async_copy(
            sources[at].at[pl.ds(part * PIECE, PIECE)], weights.at[pl.ds(slot * PIECE, PIECE)], sems.at[slot]
        )

    for slot, spots in enumerate(wanted):
        for spot in sorted(set(spots)):
            zs = [k for k, other in enumerate(spots) if other == spot]
            begin = copy(slot, spot).start
            if len(zs) == CHIPS:
                begin()
            else:
                pl.when(functools.reduce(jnp.logical_or, [z == k for k in zs]))(lambda begin=begin: begin())
    for slot, spots in enumerate(wanted):
        copy(slot, spots[0]).wait()


def project_kernel(wanted, amount, carried, info, *refs):
    refs = list(refs)
    count = len(wanted)
    wide = count > 8
    held = 1 if wide else count
    halves, refs = (refs[:held], refs[held : 2 * held]), refs[2 * held :]
    before = refs.pop(0) if carried else None
    sources, (total, token, weights, sems) = refs[:amount], refs[amount:]

    question = pl.program_id(0)

    @pl.when(question == 0)
    def _():
        load_weights(wanted, info[0], sources, weights, sems)
        token[...] = jnp.zeros_like(token)

    for half, blocks in enumerate(halves):
        rows = blocks[0].shape[1]
        here = pl.ds(half * rows, rows)
        if wide:
            places = [pl.multiple_of(info[1 + k] * PIECE, PIECE) for k in range(count)]
            found = [blocks[0][0, :, pl.ds(place, PIECE)] for place in places]
        else:
            found = [block[0] for block in blocks]
        features = jnp.concatenate(found, axis=1)
        part = jnp.dot(features, weights[...], preferred_element_type=jnp.float32)
        if carried:
            part = part + before[0, here, :]
        total[0, here, :] = part


def project_pieces(info, pieces, own_rows, other_rows, before=None):
    questions, rows, width = own_rows.shape
    columns = pieces[0][0][0][0].shape[1]
    arrays, wanted = distinct(pieces)
    count = len(pieces)
    carried = before is not None
    blocks = [pl.BlockSpec((1, rows, PIECE), lambda i, info, k=k: (i, 0, info[1 + k])) for k in range(count)]
    if count > 8:
        blocks = [pl.BlockSpec((1, rows, width), lambda i, info: (i, 0, 0))]
    held = len(blocks)
    sums = pl.BlockSpec((1, 2 * rows, columns), lambda i, info: (i, 0, 0))
    anywhere = pl.BlockSpec(memory_space=pl.ANY)
    return pl.pallas_call(
        functools.partial(project_kernel, wanted, len(arrays), carried),
        grid_spec=pltpu.PrefetchScalarGridSpec(
            num_scalar_prefetch=1,
            grid=(questions,),
            in_specs=blocks + blocks + ([sums] if carried else []) + [anywhere] * len(arrays),
            out_specs=[sums, pl.BlockSpec((8, 128), lambda i, info: (0, 0))],
            scratch_shapes=[
                pltpu.VMEM((count * PIECE, columns), jnp.bfloat16),
                pltpu.SemaphoreType.DMA((count,)),
            ],
        ),
        out_shape=[
            jax.ShapeDtypeStruct((questions, 2 * rows, columns), jnp.float32),
            jax.ShapeDtypeStruct((8, 128), jnp.float32),
        ],
        input_output_aliases={2 * held + 1: 0} if carried else {},
        compiler_params=pltpu.CompilerParams(vmem_limit_bytes=VMEM_LIMIT),
        cost_estimate=pl.CostEstimate(flops=1000, bytes_accessed=1000, transcendentals=0),
        name="project",
    )(info, *([own_rows] * held), *([other_rows] * held), *([before] if carried else []), *arrays)


def attend_kernel(wanted, amount, info, *refs):
    refs = list(refs)
    count = len(wanted)
    halves, refs = (refs[:count], refs[count : 2 * count]), refs[2 * count :]
    before, queries, live, refs = refs[0], refs[1], refs[2], refs[3:]
    sources, refs = refs[:amount], refs[amount:]
    outs, (weights, sems) = refs[:-2], refs[-2:]
    step = pl.program_id(0)

    @pl.when(step == 0)
    def _():
        load_weights(wanted, info[0], sources, weights, sems)

    found = []
    for half, blocks in enumerate(halves):
        rows = blocks[0].shape[1]
        features = jnp.concatenate([block[0] for block in blocks], axis=1)
        part = jnp.dot(features, weights[...], preferred_element_type=jnp.float32)
        found.append((part + before[0, pl.ds(half * rows, rows), :]).astype(jnp.bfloat16))
    keyval = jnp.concatenate(found, axis=0)
    width = keyval.shape[1] // 2
    answers = queries.shape[1]
    group = 4
    span = group * HD
    shown = live[0] > 0
    lane_head = lax.broadcasted_iota(jnp.int32, (answers, span), 1) // HD
    tail_lane = lax.broadcasted_iota(jnp.int32, (answers, 128), 1)
    head_total = width // HD
    extra = jnp.zeros((answers, 128), jnp.float32)
    parts = []
    for g in range(width // span):
        at = slice(g * span, (g + 1) * span)
        query = queries[0, :, at]
        spread = jnp.concatenate(
            [jnp.where(lane_head == h, query, jnp.zeros_like(query)) for h in range(group)], axis=0
        )
        scores = lax.dot_general(
            spread, keyval[:, at], (((1,), (1,)), ((), ())), preferred_element_type=jnp.float32
        )
        scores = jnp.where(shown, scores, NEGATIVE)
        peak = jnp.max(scores, axis=1, keepdims=True)
        raw = jnp.where(shown, jnp.exp(scores - peak), 0.0)
        total = jnp.sum(raw, axis=1, keepdims=True)
        value_at = slice(width + g * span, width + (g + 1) * span)
        numer = jnp.dot(raw.astype(jnp.bfloat16), keyval[:, value_at], preferred_element_type=jnp.float32)
        own = jnp.zeros((answers, span), jnp.float32)
        for h in range(group):
            mine = slice(h * answers, (h + 1) * answers)
            own = jnp.where(lane_head == h, numer[mine], own)
            extra = jnp.where(tail_lane == g * group + h, peak[mine], extra)
            extra = jnp.where(tail_lane == head_total + g * group + h, total[mine], extra)
        parts.append(own)
    result = jnp.concatenate(parts + [extra], axis=1)
    for k, out in enumerate(outs):

        @pl.when(step == k)
        def _(out=out):
            out[...] = result


def attend_last(info, pieces, own_rows, other_rows, before, queries, live, first, amount):
    questions, rows, width = own_rows.shape
    columns = pieces[0][0][0][0].shape[1]
    answers = queries.shape[1]
    arrays, wanted = distinct(pieces)
    count = len(pieces)
    wide = columns // 2 + 128

    def question(i, info):
        return lax.rem(i + first + info[0], questions)

    def turned(i, info):
        wanted = question(i, info)
        pairs = questions // 2
        return 2 * lax.rem(wanted // 2 + info[0] * (pairs - 1), pairs) + lax.rem(wanted, 2)


    blocks = [
        pl.BlockSpec((1, rows, PIECE), lambda i, info, k=k: (question(i, info), 0, info[1 + k]))
        for k in range(count)
    ]
    whole = lambda *shape: pl.BlockSpec((1,) + shape, lambda i, info: (question(i, info), 0, 0))
    anywhere = pl.BlockSpec(memory_space=pl.ANY)
    flops = 4 * amount * rows * count * PIECE * columns + 16 * amount * rows * answers * columns
    return pl.pallas_call(
        functools.partial(attend_kernel, wanted, len(arrays)),
        grid_spec=pltpu.PrefetchScalarGridSpec(
            num_scalar_prefetch=1,
            grid=(amount,),
            in_specs=blocks
            + blocks
            + [
                whole(2 * rows, columns),
                pl.BlockSpec((1, answers, columns // 2), lambda i, info: (turned(i, info), 0, 0)),
                whole(1, 2 * rows),
            ]
            + [anywhere] * len(arrays),
            out_specs=[pl.BlockSpec((answers, wide), lambda i, info: (0, 0))] * amount,
            scratch_shapes=[
                pltpu.VMEM((count * PIECE, columns), jnp.bfloat16),
                pltpu.SemaphoreType.DMA((count,)),
            ],
        ),
        out_shape=[jax.ShapeDtypeStruct((answers, wide), jnp.float32)] * amount,
        compiler_params=pltpu.CompilerParams(vmem_limit_bytes=VMEM_LIMIT),
        cost_estimate=pl.CostEstimate(
            flops=flops,
            bytes_accessed=amount * rows * (8 * columns + 4 * count * PIECE),
            transcendentals=amount * rows * answers * columns // HD,
        ),
        name="attend",
    )(info, *([own_rows] * count), *([other_rows] * count), before, queries, live, *arrays)


def merge_kernel(*refs):
    parts, out = refs[:-1], refs[-1]
    answers, width = out.shape
    heads = width // HD
    lane = lax.broadcasted_iota(jnp.int32, (answers, 128), 1)
    tails = [part[:, pl.ds(width, 128)] for part in parts]
    peak = functools.reduce(jnp.maximum, tails)
    factors = [jnp.exp(jnp.where(lane < heads, tail - peak, 0.0)) for tail in tails]

    def column(value, at):
        return value[:, at : at + 1]

    for tile in range(width // 128):
        low, high = 2 * tile, 2 * tile + 1
        numer = jnp.zeros((answers, 128), jnp.float32)
        total = jnp.zeros((answers, 128), jnp.float32)
        for part, tail, factor in zip(parts, tails, factors):
            scale = jnp.where(lane < HD, column(factor, low), column(factor, high))
            amount = jnp.where(lane < HD, column(tail, heads + low), column(tail, heads + high))
            numer += part[:, pl.ds(tile * 128, 128)] * scale
            total += amount * scale
        out[:, pl.ds(tile * 128, 128)] = (numer / total).astype(out.dtype)


def merge(parts):
    answers, wide = parts[0].shape
    return pl.pallas_call(
        merge_kernel,
        out_shape=jax.ShapeDtypeStruct((answers, wide - 128), jnp.bfloat16),
        cost_estimate=pl.CostEstimate(flops=8 * answers * wide, bytes_accessed=16 * answers * wide, transcendentals=512 * answers),
        compiler_params=pltpu.CompilerParams(vmem_limit_bytes=4 * 2**20),
        name="merge",
    )(*parts)


def hold_kernel(weights, ready, out, sem):
    copy = pltpu.make_async_copy(weights, out, sem)
    copy.start()
    copy.wait()


def hold(weights, ready):
    anywhere = pl.BlockSpec(memory_space=pl.ANY)
    return pl.pallas_call(
        hold_kernel,
        in_specs=[anywhere, anywhere],
        out_specs=pl.BlockSpec(memory_space=pltpu.VMEM),
        out_shape=pltpu.VMEM(weights.shape, weights.dtype),
        scratch_shapes=[pltpu.SemaphoreType.DMA],
        compiler_params=pltpu.CompilerParams(vmem_limit_bytes=2**20),
        cost_estimate=pl.CostEstimate(flops=0, bytes_accessed=2 * weights.size, transcendentals=0),
        name="hold",
    )(weights, ready)


def output_kernel(place, weights, first, second, out):
    width = first.shape[1]
    total = jnp.zeros(out.shape, jnp.float32)
    for part, core in ((first, place[0]), (second, 1 - place[0])):
        rows = weights[pl.ds(pl.multiple_of(core * width, width), width), :]
        total += jnp.dot(part[...], rows, preferred_element_type=jnp.float32)
    out[...] = total.astype(out.dtype)


def output_terms(place, weights, first, second):
    inside = pl.BlockSpec(memory_space=pltpu.VMEM)
    answers, columns = first.shape[0], weights.shape[1]
    return pl.pallas_call(
        output_kernel,
        in_specs=[pl.BlockSpec(memory_space=pltpu.SMEM), inside, inside, inside],
        out_specs=inside,
        out_shape=jax.ShapeDtypeStruct((answers, columns), jnp.bfloat16),
        compiler_params=pltpu.CompilerParams(vmem_limit_bytes=16 * 2**20),
        cost_estimate=pl.CostEstimate(
            flops=2 * answers * weights.size, bytes_accessed=4 * answers * columns, transcendentals=0
        ),
        name="output",
    )(place, weights, first, second)


def query_terms(states, norm_gain, query_weight):
    states_wide = states.astype(jnp.float32)
    square_part = jnp.sum(states_wide * states_wide, axis=1, keepdims=True)
    scaled = (states_wide * norm_gain.astype(jnp.float32)[None, :]).astype(jnp.bfloat16)
    query_part = jnp.dot(scaled, query_weight, preferred_element_type=jnp.float32)
    return jnp.concatenate([query_part, jnp.broadcast_to(square_part, (square_part.shape[0], 128))], axis=1)


def spread_queries(pair, questions):
    pairs = questions // 2
    spread = []
    for turn in range(pairs):
        sends = []
        for place in range(2):
            for to in range(CHIPS):
                chip = pairs * place + (to + turn) % pairs
                for core in range(2):
                    sends.append((2 * (2 * chip + core) + to // pairs, 2 * (2 * to + core) + place))
        spread.append(lax.ppermute(pair, ("pb", "fsdp"), sends))
    return spread


def gathered_shards(
    decoder_states,
    norm_gain,
    query_weight,
    key_weight,
    value_weight,
    out_weight,
    passage_states,
    block_mask,
):
    pb_index = lax.axis_index("pb")
    f = lax.axis_index("fsdp")
    z, c = pb_index // 2, pb_index % 2
    questions, rows, model_width = passage_states.shape
    width = key_weight.shape[1] // 2

    def core_columns(core):
        return jnp.concatenate(
            [lax.dynamic_slice_in_dim(w, core * width, width, 1) for w in (key_weight, value_weight)], axis=1
        )

    own = core_columns(c)
    partner = core_swap(core_columns(1 - c))
    other_rows = core_swap(passage_states)

    def info(pieces):
        return jnp.concatenate([z[None], feature_blocks(pieces, z, c, f)]).astype(jnp.int32)

    def add_pieces(pieces, sums):
        return project_pieces(info(pieces), pieces, passage_states, other_rows, sums)

    terms = query_terms(decoder_states[0], norm_gain, query_weight)

    def pair_of(both):
        query_raw, square_sum = both[:, :-128], both[:, -128:-127]
        query = (query_raw * lax.rsqrt(square_sum / model_width + 1e-06)).astype(jnp.bfloat16)
        mine = lax.dynamic_slice_in_dim(query, c * width, width, 1)
        theirs = core_swap(lax.dynamic_slice_in_dim(query, (1 - c) * width, width, 1))
        return jnp.stack([jnp.where(c == 0, mine, theirs), jnp.where(c == 0, theirs, mine)])

    blocks_here = rows // BLOCK
    mine = lax.dynamic_slice_in_dim(block_mask, f * questions, questions, 0)
    live = jnp.concatenate(
        [lax.dynamic_slice_in_dim(mine, p * blocks_here, blocks_here, 1) for p in (pb_index, pb_index ^ 1)],
        axis=1,
    )
    live = jnp.repeat(live, BLOCK, axis=1)[:, None, :]

    sums, last, queries = gather_pieces(own, partner, z, add_pieces, terms, pair_of, questions, (live,))
    queries = jnp.concatenate(queries, axis=0)


    def partials(first, amount):
        return attend_last(
            info(last), last, passage_states, other_rows, sums, queries, live, first, amount
        )

    arrived = []
    for step, part in enumerate(partials(1, CHIPS - 1), 1):
        turn = [(2 * k + core, 2 * ((k + step) % CHIPS) + core) for k in range(CHIPS) for core in range(2)]
        arrived.append(lax.ppermute(part, "pb", turn))
    arrived += partials(0, 1)
    attention = merge(arrived)

    received = []
    for flip in range(2):
        sends = [
            (2 * (2 * k + core) + x, 2 * (questions * x + k) + (core ^ flip))
            for k in range(CHIPS)
            for core in range(2)
            for x in range(2)
        ]
        received.append(lax.ppermute(attention, ("pb", "fsdp"), sends))
    partial_out = output_terms(f[None].astype(jnp.int32), hold(out_weight, attention), *received)
    other_out = lax.ppermute(partial_out, "section", [(0, 1), (1, 0)])
    summed = (partial_out.astype(jnp.float32) + other_out.astype(jnp.float32)).astype(jnp.bfloat16)
    return summed[None]


def solution(mesh):
    placed = (
        P("pb", None, "fsdp"),
        P("fsdp"),
        P("fsdp", "section"),
        P(("pb", "fsdp"), "section"),
        P(("pb", "fsdp"), "section"),
        P("section", "fsdp"),
        P("fsdp", "pb", None),
        P(),
    )
    sizes = dict(mesh.shape)
    fits = sizes == {"section": 2, "pb": 2 * CHIPS, "fsdp": 2}
    return jax.shard_map(
        gathered_shards if fits else plain_shards,
        mesh=mesh,
        in_specs=placed,
        out_specs=P("pb", None, "fsdp"),
        check_vma=False,
    )
```
